32 devices in a mesh: dp: 8 (over z, y), feat: 4 (over x, core).
Axes of the slice: x: 2, y: 2, z: 4, core: 2. Of those that a mesh axis runs over, the one named last changes fastest.
Arguments:
- fine_values: float32 [512, 8192], P('feat', 'dp'), may hold values from 0 to 1
- grad: bfloat16 [8192], P('dp'), may hold values from -6 to 6
- hess: bfloat16 [8192], P('dp'), may hold values from 0.0099487305 to 0.25
- slab_rows: int32 [8], replicated, may hold values from 256 to 1024, as said below
- split_feature: int32 [3], replicated, may hold values from 0 to 511
- split_bin: int32 [3], replicated, may hold values from 32 to 223
Outputs:
- gain: float32 [7, 512, 256], P(None, 'feat')
The draws below stay inside these ranges and needn't reach their ends.
Inputs may be any that keep to these rules, and one draw needn't show every extreme that they name: `slab_rows`: each slab's used rows are its first ones; the fullest slab uses all 1024 slots.
All inputs are finite; a program needn't handle non-finite values.
Results may differ from the reference program's by a relative error of at most 0.0003.
Values sent between devices are 32-bit elements; how exact they have to be, the bound alone decides.
No kernel may reach another device: no remote copies, remote signals or barrier semaphores. Data moves between devices by JAX's collectives and lax.ppermute only.
A program may use at most 64 MiB of HBM per device.

```python
import math
import jax
import jax.numpy as jnp
from jax import lax

FEATURES = 512
FINE_BINS = 1024
BINS = 256
LEVELS = 3
ROW_DEV = 1024
ROWS = 8192
NODES = 7
INNER = 3
N_DP = 8


def draw_slab_rows(key, part):
    key = jax.random.fold_in(key, 11)
    first_key, second_key = jax.random.split(key)
    counts = jax.random.randint(first_key, (N_DP,), ROW_DEV // 4, ROW_DEV + 1)
    fullest = jax.random.randint(second_key, (), 0, N_DP)
    return jnp.where(jnp.arange(N_DP) == fullest, ROW_DEV, counts).astype(jnp.int32)


def draw_fine_values(key, part):
    key = jax.random.fold_in(key, 5)
    return jax.random.uniform(key, (FEATURES, ROWS), jnp.float32, 0.0, 1.0)


def levels(own_key, extent, shards, low, largest):
    level, own = 1.0, jax.random.fold_in(own_key, 6)
    for axis_at, shards_of in shards:
        draws = jnp.exp(jax.random.uniform(jax.random.fold_in(own, axis_at), (shards_of,), jnp.float32, low / len(shards), largest / len(shards)))
        level = level * jnp.repeat(draws, extent[axis_at] // shards_of).reshape([-1 if axis == axis_at else 1 for axis in range(len(extent))])
    return level


def noise(stream_key, dims, width, bound, cuts=(), held_as=jnp.bfloat16):
    values = jax.random.normal(stream_key, dims, jnp.float32) * width
    if len(cuts) > 0:
        values = levels(stream_key, dims, cuts, -0.22, 0.18) * values
    return jnp.clip(values, min=-bound, max=bound).astype(held_as)


def setup_inputs(seed: int = 0) -> dict:
    key_of = jax.random.split(jax.random.key(seed), 7)
    return {
        "fine_values": draw_fine_values(jax.random.fold_in(key_of[6], 71), 0),
        "grad": noise(key_of[1], (ROWS,), 1.0, 6.0, ((0, 8),)),
        "hess": jnp.clip(jnp.exp(math.log(0.25) - 3.224016 * jax.random.uniform(key_of[2], (ROWS,), jnp.float32) ** levels(key_of[2], (ROWS,), ((0, 8),), -0.2, 0.2)), 0.0099487305, 0.25).astype(jnp.bfloat16),
        "slab_rows": draw_slab_rows(jax.random.fold_in(key_of[6], 71), 0),
        "split_feature": jax.random.randint(key_of[4], (INNER,), 0, FEATURES).astype(jnp.int32),
        "split_bin": jax.random.randint(key_of[5], (INNER,), 32, 224).astype(jnp.int32),
    }


penalty = 1.0


def fine_of(values_now):
    return jnp.clip(jnp.floor(values_now * FINE_BINS), 0, FINE_BINS - 1).astype(jnp.int32)


def quantile_cut(before, total):
    remainder = before
    quotient = jnp.zeros_like(before)
    for step_now in range(BINS.bit_length() - 1):
        remainder = remainder * 2
        bit_now = remainder >= total
        remainder = jnp.where(bit_now, remainder - total, remainder).astype(jnp.int32)
        quotient = (quotient * 2 + bit_now.astype(jnp.int32)).astype(jnp.int32)
    return jnp.minimum(BINS - 1, quotient).astype(jnp.int32)


def coarse_map(counts):
    whole_counts = (counts * 16384.0).astype(jnp.int32)
    before = (jnp.cumsum(whole_counts, axis=1, dtype=jnp.int32) - whole_counts).astype(jnp.int32)
    total = jnp.sum(whole_counts, axis=1, keepdims=True, dtype=jnp.int32)
    return quantile_cut(before, total)


def gains_of(full_hist):
    totals = jnp.sum(full_hist, axis=3, keepdims=True)
    left_sums = jnp.cumsum(full_hist, axis=3)
    rights = totals - left_sums

    def score_of(sums_part):
        return sums_part[:, 0] ** 2 / (sums_part[:, 1] + penalty)

    return score_of(left_sums) + score_of(rights) - score_of(totals)


def reference(fine_values, grad, hess, slab_rows, split_feature, split_bin):
    rows_all = fine_values.shape[1]
    row_ids = jnp.arange(rows_all, dtype=jnp.int32)
    live_rows = (row_ids % ROW_DEV) < slab_rows[row_ids // ROW_DEV]
    fine_bins = fine_of(fine_values)
    weights = jnp.where(live_rows, hess.astype(jnp.float32), jnp.float32(0.0))

    def count_row(fine_row):
        return jax.ops.segment_sum(weights, fine_row, num_segments=FINE_BINS)

    counts = lax.map(count_row, fine_bins)
    map_table = coarse_map(counts)
    coarse = jnp.take_along_axis(map_table, fine_bins, axis=1)
    node_now = jnp.where(live_rows, 0, -1).astype(jnp.int32)
    node_levels = [node_now]
    for depth_now in range(1, LEVELS):
        safe_node = jnp.clip(node_now, 0, INNER - 1)
        feat_row = split_feature[safe_node]
        bin_row = split_bin[safe_node]
        picked = jnp.take_along_axis(coarse, feat_row[None, :], 0)[0]
        went_left = picked <= bin_row
        node_now = jnp.where(node_now >= 0, 2 * node_now + jnp.where(went_left, 1, 2), -1).astype(jnp.int32)
        node_levels.append(node_now)
    pair_rows = jnp.stack([grad, hess]).astype(jnp.float32).T
    full_hist = jnp.zeros((NODES, 2, FEATURES, BINS), jnp.float32)
    for nodes_row in node_levels:
        segment_ids = jnp.where(nodes_row >= 0, nodes_row, NODES)
        bin_ids = segment_ids[None, :] * BINS + coarse

        def per_feature(ids_row):
            return jax.ops.segment_sum(pair_rows, ids_row, num_segments=(NODES + 1) * BINS)

        table_now = lax.map(per_feature, bin_ids)
        table_now = table_now.reshape(FEATURES, NODES + 1, BINS, 2)[:, :NODES]
        full_hist = full_hist + jnp.transpose(table_now, (1, 3, 0, 2))
    return gains_of(full_hist)
```

```python
import jax
import jax.numpy as jnp
from jax import lax
from jax.experimental import pallas as pl
from jax.experimental.pallas import tpu as pltpu
from jax.sharding import PartitionSpec as P

FINE_BINS=1024; BINS=256; HI=8; LO=128; CHUNK=256
f32=jnp.float32; bf16=jnp.bfloat16; i32=jnp.int32

def dot_nt(a,b):
    return lax.dot_general(a,b,(((1,),(1,)),((),())),preferred_element_type=f32)

def running_sum(whole):
    n=whole.shape[0]
    lane=lax.broadcasted_iota(i32,(n,LO),1)
    sub=lax.broadcasted_iota(i32,(n,LO),0)%HI
    x=whole
    for s in (1,2,4,8,16,32,64):
        x=x+jnp.where(lane>=s,pltpu.roll(x,s,1),0)
    tot=jnp.broadcast_to(x[:,LO-1:LO],(n,LO))
    y=tot
    for s in (1,2,4):
        y=y+jnp.where(sub>=s,pltpu.roll(y,s,0),0)
    return x+(y-tot), y

def coarse_of(whole):
    n=whole.shape[0]
    incl,rows=running_sum(whole)
    before=incl-whole
    g=rows.reshape(n//HI,HI,LO)
    total=jnp.broadcast_to(g[:,HI-1:HI,:],(n//HI,HI,LO)).reshape(n,LO)
    rem=before; quo=jnp.zeros_like(before)
    for _ in range(8):
        rem=rem*2
        bit=rem>=total
        rem=jnp.where(bit,rem-total,rem)
        quo=quo*2+bit.astype(i32)
    return jnp.minimum(BINS-1,quo)

def parts_of(v):
    t=jnp.clip(jnp.floor(v*FINE_BINS),0,FINE_BINS-1)
    hi=jnp.floor(t*(1.0/LO))
    return t,hi,t-hi*LO

def make_kernel(n_dp,feats,row_dev):
  def kernel(slab_rows,split_bin,order,x_ref,s_ref,o_ref,acc_ref,cum_ref):
    sub16=lax.broadcasted_iota(i32,(16,CHUNK),0)
    k16=(sub16%HI).astype(f32).astype(bf16)
    m16=[(sub16+16*j).astype(f32).astype(bf16) for j in range(LO//16)]
    one=jnp.ones((16,CHUNK),bf16); zero=jnp.zeros((16,CHUNK),bf16)
    def lower_hot(lo_row):
        lb=jnp.broadcast_to(lo_row,(16,CHUNK)).astype(bf16)
        return jnp.concatenate([jnp.where(lb==m,one,zero) for m in m16],0)
    def chunks(s):
        return (slab_rows[s]+CHUNK-1)//CHUNK
    cnt=tuple(jnp.zeros((HI,LO),f32) for _ in range(3))
    for s in range(n_dp):
        def body(q,cnt,s=s):
            r0=pl.multiple_of(q*CHUNK,CHUNK)
            rows=s_ref[order[s],:,pl.ds(r0,CHUNK)]
            live=lax.broadcasted_iota(i32,(1,CHUNK),1)+r0<slab_rows[s]
            h=jnp.where(live,rows[1:2],0.0)
            hb=jnp.broadcast_to(h,(16,CHUNK)).astype(bf16)
            t,hi,lo=parts_of(rows)
            out=[]
            for n in range(3):
                kb=jnp.broadcast_to(hi[2+n:3+n],(16,CHUNK)).astype(bf16)
                a=jnp.where(kb==k16,hb,zero)
                out.append(cnt[n]+dot_nt(a,lower_hot(lo[2+n:3+n]))[:HI])
            return tuple(out)
        cnt=lax.fori_loop(0,chunks(s),body,cnt)
    whole=(jnp.concatenate(cnt,0)*16384.0).astype(i32)
    cut=coarse_of(whole)
    thr=[]
    for n in range(3):
        left=(cut[n*HI:(n+1)*HI]<=split_bin[n]).astype(f32)
        thr.append(jnp.sum(jnp.sum(left,axis=0,keepdims=True),axis=1,keepdims=True))
    acc_ref[...]=jnp.zeros_like(acc_ref)
    sub8=lax.broadcasted_iota(i32,(8,CHUNK),0)
    for s in range(n_dp):
        def body(q,_,s=s):
            r0=pl.multiple_of(q*CHUNK,CHUNK)
            rows=s_ref[order[s],:,pl.ds(r0,CHUNK)]
            live=lax.broadcasted_iota(i32,(1,CHUNK),1)+r0<slab_rows[s]
            g=jnp.where(live,rows[0:1],0.0); h=jnp.where(live,rows[1:2],0.0)
            t,_,_=parts_of(rows)
            l0=t[2:3]<thr[0]; l1=t[3:4]<thr[1]; l2=t[4:5]<thr[2]
            leaf=jnp.where(l0,jnp.where(l1,0,1),jnp.where(l2,2,3))
            gh=jnp.where(sub8<4,jnp.broadcast_to(g,(8,CHUNK)),jnp.broadcast_to(h,(8,CHUNK)))
            ch=jnp.where((sub8%4)==jnp.broadcast_to(leaf,(8,CHUNK)),gh,0.0)
            ch2=jnp.concatenate([ch,ch],0).astype(bf16)
            x=x_ref[s,:,pl.ds(r0,CHUNK)]
            _,hi,lo=parts_of(x)
            kk=[(sub16//8+2*j).astype(f32).astype(bf16) for j in range(4)]
            for f in range(feats):
                hb=jnp.broadcast_to(hi[f:f+1],(16,CHUNK)).astype(bf16)
                a=jnp.concatenate([jnp.where(hb==kk[j],ch2,zero) for j in range(4)],0)
                acc_ref[f]+=dot_nt(a,lower_hot(lo[f:f+1]))
            return 0
        lax.fori_loop(0,chunks(s),body,0)
    acc=acc_ref[...].reshape(feats*HI,8,LO)
    is_h=lax.broadcasted_iota(i32,(feats*HI,8,LO),1)>=4
    cnts=jnp.sum(jnp.where(is_h,acc,0.0),axis=1)
    cut=coarse_of((cnts*16384.0).astype(i32)).astype(f32)
    b16=lax.broadcasted_iota(i32,(16,LO),0)
    one2=jnp.ones((16,LO),bf16); zero2=jnp.zeros((16,LO),bf16)
    bs=[(b16+16*j).astype(f32).astype(bf16) for j in range(BINS//16)]
    for f in range(feats):
        left=[];right=[]
        for k in range(HI):
            fk=acc_ref[f,k*8:(k+1)*8,:]
            p0=fk.astype(bf16); r1=fk-p0.astype(f32); p1=r1.astype(bf16); p2=(r1-p1.astype(f32)).astype(bf16)
            left.append(jnp.concatenate([p0.astype(f32),p1.astype(f32),p2.astype(f32),jnp.zeros((8,LO),f32)],0).astype(bf16))
            cb=jnp.broadcast_to(cut[f*HI+k:f*HI+k+1],(16,LO)).astype(bf16)
            right.append(jnp.concatenate([jnp.where(cb<=b,one2,zero2) for b in bs],0))
        r=dot_nt(jnp.concatenate(left,1),jnp.concatenate(right,1))
        gl=(r[0:8]+r[8:16])+r[16:24]
        for c in range(8):
            cum_ref[c,f:f+1,:]=gl[c:c+1]
    def score(g,h):
        return g*g/(h+1.0)
    gs=[cum_ref[c] for c in range(4)]; hs=[cum_ref[4+c] for c in range(4)]
    def nodes(l):
        a=l[0]+l[1]; b=l[2]+l[3]
        return [a+b,a,b]+l
    for n,(gl,hl) in enumerate(zip(nodes(gs),nodes(hs))):
        gt=gl[:,BINS-1:BINS]; ht=hl[:,BINS-1:BINS]
        o_ref[n]=score(gl,hl)+score(gt-gl,ht-hl)-score(gt,ht)
  return kernel

def histogram_gains(x,s,slab_rows,split_bin,order):
    n_dp,feats,row_dev=x.shape
    smem=pl.BlockSpec(memory_space=pltpu.SMEM); vm=pl.BlockSpec(memory_space=pltpu.VMEM)
    return pl.pallas_call(make_kernel(n_dp,feats,row_dev),
      out_shape=jax.ShapeDtypeStruct((7,feats,BINS),f32),
      in_specs=[smem,smem,smem,vm,vm],out_specs=vm,
      scratch_shapes=[pltpu.VMEM((feats,64,LO),f32),pltpu.VMEM((8,feats,BINS),f32)],
      compiler_params=pltpu.CompilerParams(vmem_limit_bytes=32*2**20),
      name="gains")(slab_rows,split_bin,order,x,s)


def swap(value, axis, size, step):
    return lax.ppermute(value, axis, [(s, s ^ step) for s in range(size)])


def make_shards(n_dp, n_feat):
    def shards(fine_values, grad, hess, slab_rows, split_feature, split_bin):
        feat_dev, row_dev = fine_values.shape
        feats = feat_dev // n_dp
        me = lax.axis_index("dp")
        local = split_feature - lax.axis_index("feat") * feat_dev
        owned = (local >= 0) & (local < feat_dev)
        at = jnp.clip(local, 0, feat_dev - 1)
        picked = jnp.concatenate([lax.dynamic_slice_in_dim(fine_values, at[n], 1, 0) for n in range(3)])
        picked = jnp.where(owned[:, None], picked, 0.0)
        step = 1
        while step < n_feat:
            picked = picked + swap(picked, "feat", n_feat, step)
            step *= 2
        rows = jnp.concatenate([grad.astype(f32)[None], hess.astype(f32)[None], picked, jnp.zeros((3, row_dev), f32)])[None]
        step = 1
        while step < n_dp:
            rows = jnp.concatenate([rows, swap(rows, "dp", n_dp, step)])
            step *= 2
        blocks = lax.all_to_all(fine_values.reshape(n_dp, feats, row_dev), "dp", 0, 0)
        order = jnp.arange(n_dp, dtype=i32) ^ me
        gains = histogram_gains(blocks, rows, slab_rows, split_bin, order)
        whole = jnp.zeros((7, feat_dev, BINS), f32)
        for d in range(n_dp):
            piece = gains if d == 0 else swap(gains, "dp", n_dp, d)
            whole = lax.dynamic_update_slice_in_dim(whole, piece, (me ^ d) * feats, 1)
        return whole

    return shards


def solution(mesh):
    return jax.shard_map(
        make_shards(mesh.shape["dp"], mesh.shape["feat"]),
        mesh=mesh,
        in_specs=(P("feat", "dp"), P("dp"), P("dp"), P(), P(), P()),
        out_specs=P(None, "feat", None),
        check_vma=False,
    )
```

```python
import jax
import jax.numpy as jnp
from jax import lax
from jax.experimental import pallas as pl
from jax.experimental.pallas import tpu as pltpu
from jax.sharding import PartitionSpec as P

FINE_BINS = 1024
BINS = 256
HI = 8
LO = 128
CHUNK = 256
GROUP = 4
f32 = jnp.float32
bf16 = jnp.bfloat16
i32 = jnp.int32


def dot_nt(a, b):
    return lax.dot_general(a, b, (((1,), (1,)), ((), ())), preferred_element_type=f32)


def dot_nn(a, b):
    return jnp.dot(a, b, preferred_element_type=f32)


def iota(shape, axis):
    return lax.broadcasted_iota(i32, shape, axis)


def to_bf16(x):
    return x.astype(f32).astype(bf16)


def bytes_of(x, axis):
    return jnp.concatenate([to_bf16((x >> (8 * i)) & 255) for i in range(4)], axis)


def coarse_of(whole, group):
    n = whole.shape[0]
    r, c = iota((LO, 2 * LO), 0), iota((LO, 2 * LO), 1)
    in_row = dot_nn(bytes_of(whole, 0), to_bf16((r < c) | (c >= LO)))
    in_row = in_row.astype(i32)
    in_row = sum(in_row[i * n : (i + 1) * n] << (8 * i) for i in range(4))
    before, row_total = in_row[:, :LO], in_row[:, LO:]
    r, c = iota((2 * n, n), 0), iota((2 * n, n), 1)
    same = (r % n) // group == c // group
    over = dot_nn(to_bf16(same & ((c < r) | (r >= n))), bytes_of(row_total, 1)).astype(i32)
    over = sum(over[:, i * LO : (i + 1) * LO] << (8 * i) for i in range(4))
    total = over[n:]
    remainder = before + over[:n]
    quotient = jnp.zeros_like(remainder)
    for _ in range(BINS.bit_length() - 1):
        remainder = remainder * 2
        bit = remainder >= total
        remainder = jnp.where(bit, remainder - total, remainder)
        quotient = quotient * 2 + bit.astype(i32)
    return jnp.minimum(BINS - 1, quotient)


def fine_of(v):
    return jnp.clip(jnp.floor(v * FINE_BINS), 0, FINE_BINS - 1)


def hi_lo(t):
    hi = jnp.floor(t * (1.0 / LO))
    return hi, t - hi * LO


def hot(row, rows, width):
    b = jnp.broadcast_to(row, (16, width)).astype(bf16)
    at = iota((16, width), 0)
    one, zero = jnp.ones((16, width), bf16), jnp.zeros((16, width), bf16)
    return jnp.concatenate([jnp.where(b == to_bf16(at + 16 * j), one, zero) for j in range(rows // 16)], 0)


def make_route(n_dp, row_dev):
    tiles = row_dev // LO
    side = 32

    def kernel(slab_rows, split_bin, *refs):
        blocks, ch_ref, t_ref = refs[: n_dp // 2], refs[n_dp // 2], refs[n_dp // 2 + 1]
        me = lax.axis_index("dp")
        at16 = iota((16, LO), 0)
        steps = [to_bf16(at16), to_bf16(at16 + 16)]
        one, zero = jnp.ones((16, LO), bf16), jnp.zeros((16, LO), bf16)
        counts = [jnp.zeros((side, side), f32) for _ in range(3)]
        for j in range(n_dp):
            block = blocks[j // 2]
            row = iota((tiles, LO), 0) * LO + iota((tiles, LO), 1)
            live = row < slab_rows[me ^ j]
            t_ref[j, 3] = jnp.where(live, block[j % 2, 3 * tiles : 4 * tiles], 0.0)
            h = jnp.where(live, block[j % 2, 4 * tiles :], 0.0)
            t_ref[j, 4] = h
            hs = [jnp.broadcast_to(h[i : i + 1], (16, LO)).astype(bf16) for i in range(tiles)]
            for n in range(3):
                t = fine_of(block[j % 2, n * tiles : (n + 1) * tiles])
                t_ref[j, n] = t
                hi = jnp.floor(t * (1.0 / side))
                lo = t - hi * side
                left, right = [], []
                for i in range(tiles):
                    hb = jnp.broadcast_to(hi[i : i + 1], (16, LO)).astype(bf16)
                    lb = jnp.broadcast_to(lo[i : i + 1], (16, LO)).astype(bf16)
                    left.append(jnp.concatenate([jnp.where(hb == k, hs[i], zero) for k in steps], 0))
                    right.append(jnp.concatenate([jnp.where(lb == k, one, zero) for k in steps], 0))
                counts[n] += dot_nt(jnp.concatenate(left, 1), jnp.concatenate(right, 1))
        whole = (jnp.concatenate(counts, 0) * 16384.0).astype(i32)
        cut = coarse_of(jnp.concatenate([whole, jnp.zeros((3 * side, LO - side), i32)], 1), side)
        cuts = []
        for n in range(3):
            below = (cut[n * side : (n + 1) * side] <= split_bin[n]) & (iota((side, LO), 1) < side)
            below = jnp.where(below, 1.0, 0.0)
            cuts.append(jnp.sum(jnp.sum(below, axis=0, keepdims=True), axis=1, keepdims=True))
        ch_ref[n_dp] = jnp.zeros((8, row_dev), f32)
        at = iota((8, LO), 0)
        for j in range(n_dp):
            s = me ^ j
            l0, l1, l2 = [t_ref[j, n] < cuts[n] for n in range(3)]
            leaf = jnp.where(l0, jnp.where(l1, 0, 1), jnp.where(l2, 2, 3))
            g, h = t_ref[j, 3], t_ref[j, 4]
            for i in range(tiles):
                gh = jnp.where(at < 4, jnp.broadcast_to(g[i : i + 1], (8, LO)), jnp.broadcast_to(h[i : i + 1], (8, LO)))
                here = at % 4 == jnp.broadcast_to(leaf[i : i + 1], (8, LO))
                ch_ref[s, :, i * LO : (i + 1) * LO] = jnp.where(here, gh, 0.0)

    return kernel


def route_rows(blocks, slab_rows, split_bin, n_dp, row_dev):
    smem = pl.BlockSpec(memory_space=pltpu.SMEM)
    vmem = pl.BlockSpec(memory_space=pltpu.VMEM)
    return pl.pallas_call(
        make_route(n_dp, row_dev),
        out_shape=jax.ShapeDtypeStruct((n_dp + 1, 8, row_dev), f32),
        in_specs=[smem, smem] + [vmem] * len(blocks),
        out_specs=vmem,
        scratch_shapes=[pltpu.VMEM((n_dp, 5, row_dev // LO, LO), f32)],
        compiler_params=pltpu.CompilerParams(vmem_limit_bytes=32 * 2**20),
        cost_estimate=pl.CostEstimate(flops=2 * 96 * 256 * n_dp * row_dev, bytes_accessed=2**18, transcendentals=0),
        name="route",
    )(slab_rows, split_bin, *blocks)


def make_gains(n_dp, feats, row_dev):
    pairs = feats // 2
    per = row_dev // CHUNK
    width = GROUP * CHUNK

    def kernel(slab_rows, x_ref, ch_ref, o_ref, list_ref, acc_ref, cum_ref):
        def note(i, n):
            list_ref[n] = i
            return n + (i % per * CHUNK < slab_rows[i // per]).astype(i32)

        used = lax.fori_loop(0, n_dp * per, note, 0)
        for i in range(GROUP - 1):
            list_ref[used + i] = n_dp * per
        acc_ref[...] = jnp.zeros_like(acc_ref)
        kk = [to_bf16(iota((16, width), 0) // 8 + 2 * j) for j in range(HI // 2)]
        zero = jnp.zeros((16, width), bf16)
        in_first = iota((LO, LO), 1) < 64

        def add(q, _):
            xs, chs = [], []
            for i in range(GROUP):
                at = list_ref[q * GROUP + i]
                s = at // per
                col = pl.ds(pl.multiple_of((at % per) * CHUNK, CHUNK), CHUNK)
                xs.append(x_ref[jnp.minimum(s, n_dp - 1), :, col])
                chs.append(ch_ref[s, :, col])
            ch = jnp.concatenate(chs, 1)
            ch = jnp.concatenate([ch, ch], 0).astype(bf16)
            hi, lo = hi_lo(fine_of(jnp.concatenate(xs, 1)))

            def spread(f):
                hb = jnp.broadcast_to(hi[f : f + 1], (16, width)).astype(bf16)
                return [jnp.where(hb == k, ch, zero) for k in kk]

            for p in range(pairs):
                f = 2 * p
                w = jnp.concatenate(spread(f) + spread(f + 1), 0)
                a = dot_nt(hot(lo[f : f + 1], LO, width), w)
                b = dot_nt(hot(lo[f + 1 : f + 2], LO, width), w)
                acc_ref[p] += jnp.where(in_first, a, b)
            return 0

        lax.fori_loop(0, (used + GROUP - 1) // GROUP, add, 0)
        n = feats * HI
        acc = jnp.concatenate([jnp.transpose(acc_ref[p]) for p in range(pairs)], 0)
        p0 = acc.astype(bf16)
        r1 = acc - p0.astype(f32)
        p1 = r1.astype(bf16)
        r2 = r1 - p1.astype(f32)
        r, c = iota((n, n * 8), 0), iota((n, n * 8), 1)
        pick = to_bf16((c // 8 == r) & (c % 8 >= 4))
        counts = (dot_nn(pick, p0) + dot_nn(pick, p1)) + dot_nn(pick, r2.astype(bf16))
        cut = coarse_of((counts * 16384.0).astype(i32), HI).astype(f32)
        edges = [to_bf16(iota((16, LO), 0) + 16 * j) for j in range(BINS // 16)]
        one, none = jnp.ones((16, LO), bf16), jnp.zeros((16, LO), bf16)
        q0, q1 = p0.astype(f32), p1.astype(f32)
        sums = []
        for f in range(feats):
            left, right = [], []
            for k in range(HI):
                at = f * HI + k
                cb = jnp.broadcast_to(cut[at : at + 1], (16, LO)).astype(bf16)
                left.append(jnp.concatenate([jnp.where(cb <= e, one, none) for e in edges], 0))
                right.append(jnp.concatenate([q0[at * 8 : at * 8 + 8], q1[at * 8 : at * 8 + 8]], 0).astype(bf16))
            sums.append(dot_nt(jnp.concatenate(left, 1), jnp.concatenate(right, 1)))
        per_tile = LO // 16
        for f0 in range(0, feats, per_tile):
            tile = jnp.concatenate(sums[f0 : f0 + per_tile], 1)
            if tile.shape[1] < LO:
                tile = jnp.concatenate([tile, jnp.zeros((BINS, LO - tile.shape[1]), f32)], 1)
            tile = jnp.transpose(tile)
            for f in range(f0, min(f0 + per_tile, feats)):
                at = (f - f0) * 16
                gl = tile[at : at + 8] + tile[at + 8 : at + 16]
                for c in range(8):
                    cum_ref[c, f : f + 1, :] = gl[c : c + 1]

        def score(g, h):
            return g * g / (h + 1.0)

        def nodes(first):
            leaves = [cum_ref[first + c] for c in range(4)]
            a, b = leaves[0] + leaves[1], leaves[2] + leaves[3]
            return [a + b, a, b] + leaves

        for i, (gl, hl) in enumerate(zip(nodes(0), nodes(4))):
            g, h = gl[:, BINS - 1 :], hl[:, BINS - 1 :]
            o_ref[i] = score(gl, hl) + score(g - gl, h - hl) - score(g, h)

    return kernel


def gains_of(x, ch, slab_rows):
    n_dp, feats, row_dev = x.shape
    smem = pl.BlockSpec(memory_space=pltpu.SMEM)
    vmem = pl.BlockSpec(memory_space=pltpu.VMEM)
    return pl.pallas_call(
        make_gains(n_dp, feats, row_dev),
        out_shape=jax.ShapeDtypeStruct((7, feats, BINS), f32),
        in_specs=[smem, vmem, vmem],
        out_specs=vmem,
        scratch_shapes=[
            pltpu.SMEM((n_dp * (row_dev // CHUNK) + GROUP,), i32),
            pltpu.VMEM((feats // 2, LO, LO), f32),
            pltpu.VMEM((8, feats, BINS), f32),
        ],
        compiler_params=pltpu.CompilerParams(vmem_limit_bytes=40 * 2**20),
        cost_estimate=pl.CostEstimate(flops=2 * 128 * 256 * n_dp * row_dev * feats, bytes_accessed=2**20, transcendentals=0),
        name="gains",
    )(slab_rows, x, ch)


def make_pick(feat_dev, row_dev):
    tiles = row_dev // LO

    def kernel(split_feature, x_ref, o_ref, rows_ref, sems):
        me = lax.axis_index("feat")
        work = []
        for n in range(3):
            local = split_feature[n] - me * feat_dev
            owned = (local >= 0) & (local < feat_dev)
            at = jnp.clip(local, 0, feat_dev - 1)
            first = pl.multiple_of(at // 8 * 8, 8)
            copy = pltpu.make_async_copy(x_ref.at[pl.ds(first, 8), :], rows_ref.at[n], sems.at[n])
            copy.start()
            work.append((copy, at % 8, jnp.where(owned, 1.0, 0.0)))
        for n, (copy, at, scale) in enumerate(work):
            copy.wait()
            row = jnp.where(iota((8, row_dev), 0) == at, rows_ref[n], 0.0)
            row = jnp.sum(row, axis=0, keepdims=True) * scale
            for i in range(tiles):
                o_ref[n * tiles + i : n * tiles + i + 1, :] = row[:, i * LO : (i + 1) * LO]

    return kernel


def pick_rows(fine_values, split_feature):
    feat_dev, row_dev = fine_values.shape
    return pl.pallas_call(
        make_pick(feat_dev, row_dev),
        out_shape=jax.ShapeDtypeStruct((3 * row_dev // LO, LO), f32),
        in_specs=[pl.BlockSpec(memory_space=pltpu.SMEM), pl.BlockSpec(memory_space=pl.ANY)],
        out_specs=pl.BlockSpec(memory_space=pltpu.VMEM),
        scratch_shapes=[pltpu.VMEM((3, 8, row_dev), f32), pltpu.SemaphoreType.DMA((3,))],
        name="pick",
    )(split_feature, fine_values)


def swap(value, axis, size, step):
    return lax.ppermute(value, axis, [(s, s ^ step) for s in range(size)])


def make_shards(n_dp, n_feat):
    def shards(fine_values, grad, hess, slab_rows, split_feature, split_bin):
        feat_dev, row_dev = fine_values.shape
        feats = feat_dev // n_dp
        me = lax.axis_index("dp")
        both = ("dp", "feat")
        share = pick_rows(fine_values, split_feature)
        share = share + swap(share, "feat", n_feat, 1)
        gh = jnp.concatenate([grad.astype(f32).reshape(-1, LO), hess.astype(f32).reshape(-1, LO)])
        block = jnp.concatenate([share, gh])
        mine, other = share, swap(block, "dp", n_dp, 1)
        v, other_gh = other[: share.shape[0]], other[share.shape[0] :]
        for x in range(2, n_feat, 2):
            mine = mine + swap(share, "feat", n_feat, x)
            v = v + swap(share, both, n_dp * n_feat, n_feat + x)
        pair = jnp.stack([jnp.concatenate([mine, gh]), jnp.concatenate([v, other_gh])])
        pairs = [pair] + [swap(pair, "dp", n_dp, d) for d in range(2, n_dp, 2)]
        blocks = lax.all_to_all(fine_values.reshape(n_dp, feats, row_dev), "dp", 0, 0)
        ch = route_rows(pairs, slab_rows, split_bin, n_dp, row_dev)
        gains = gains_of(blocks, ch, slab_rows)
        whole = jnp.zeros((7, feat_dev, BINS), f32)
        for d in range(n_dp):
            piece = gains if d == 0 else swap(gains, "dp", n_dp, d)
            whole = lax.dynamic_update_slice_in_dim(whole, piece, (me ^ d) * feats, 1)
        return whole

    return shards


def solution(mesh):
    return jax.shard_map(
        make_shards(mesh.shape["dp"], mesh.shape["feat"]),
        mesh=mesh,
        in_specs=(P("feat", "dp"), P("dp"), P("dp"), P(), P(), P()),
        out_specs=P(None, "feat", None),
        check_vma=False,
    )
```

```python
import jax
import jax.numpy as jnp
from jax import lax
from jax.experimental import pallas as pl
from jax.experimental.pallas import tpu as pltpu
from jax.sharding import PartitionSpec as P

FINE_BINS = 1024
BINS = 256
HI = 8
LO = 128
CHUNK = 256
GROUP = 4
f32 = jnp.float32
bf16 = jnp.bfloat16
i32 = jnp.int32


def dot_nt(a, b):
    return lax.dot_general(a, b, (((1,), (1,)), ((), ())), preferred_element_type=f32)


def dot_nn(a, b):
    return jnp.dot(a, b, preferred_element_type=f32)


def iota(shape, axis):
    return lax.broadcasted_iota(i32, shape, axis)


def to_bf16(x):
    return x.astype(f32).astype(bf16)


def bytes_of(x, axis):
    return jnp.concatenate([to_bf16((x >> (8 * i)) & 255) for i in range(4)], axis)


def coarse_of(whole, group):
    n = whole.shape[0]
    r, c = iota((LO, 2 * LO), 0), iota((LO, 2 * LO), 1)
    in_row = dot_nn(bytes_of(whole, 0), to_bf16((r < c) | (c >= LO)))
    in_row = in_row.astype(i32)
    in_row = sum(in_row[i * n : (i + 1) * n] << (8 * i) for i in range(4))
    before, row_total = in_row[:, :LO], in_row[:, LO:]
    r, c = iota((2 * n, n), 0), iota((2 * n, n), 1)
    same = (r % n) // group == c // group
    over = dot_nn(to_bf16(same & ((c < r) | (r >= n))), bytes_of(row_total, 1)).astype(i32)
    over = sum(over[:, i * LO : (i + 1) * LO] << (8 * i) for i in range(4))
    total = over[n:]
    remainder = before + over[:n]
    quotient = jnp.zeros_like(remainder)
    for _ in range(BINS.bit_length() - 1):
        remainder = remainder * 2
        bit = remainder >= total
        remainder = jnp.where(bit, remainder - total, remainder)
        quotient = quotient * 2 + bit.astype(i32)
    return jnp.minimum(BINS - 1, quotient)


def fine_of(v):
    return jnp.clip(jnp.floor(v * FINE_BINS), 0, FINE_BINS - 1)


def hi_lo(t):
    hi = jnp.floor(t * (1.0 / LO))
    return hi, t - hi * LO


def hot(row, rows, width):
    b = jnp.broadcast_to(row, (16, width)).astype(bf16)
    at = iota((16, width), 0)
    one, zero = jnp.ones((16, width), bf16), jnp.zeros((16, width), bf16)
    return jnp.concatenate([jnp.where(b == to_bf16(at + 16 * j), one, zero) for j in range(rows // 16)], 0)


def make_route(n_dp, row_dev):
    tiles = row_dev // LO
    side = 32

    def kernel(slab_rows, split_bin, *refs):
        blocks, ch_ref, t_ref = refs[: n_dp // 2], refs[n_dp // 2], refs[n_dp // 2 + 1]
        me = lax.axis_index("dp")
        at16 = iota((16, LO), 0)
        steps = [to_bf16(at16), to_bf16(at16 + 16)]
        one, zero = jnp.ones((16, LO), bf16), jnp.zeros((16, LO), bf16)
        counts = [jnp.zeros((side, side), f32) for _ in range(3)]
        for j in range(n_dp):
            block = blocks[j // 2]
            row = iota((tiles, LO), 0) * LO + iota((tiles, LO), 1)
            live = row < slab_rows[me ^ j]
            t_ref[j, 3] = jnp.where(live, block[j % 2, 3 * tiles : 4 * tiles], 0.0)
            h = jnp.where(live, block[j % 2, 4 * tiles :], 0.0)
            t_ref[j, 4] = h
            hs = [jnp.broadcast_to(h[i : i + 1], (16, LO)).astype(bf16) for i in range(tiles)]
            for n in range(3):
                t = fine_of(block[j % 2, n * tiles : (n + 1) * tiles])
                t_ref[j, n] = t
                hi = jnp.floor(t * (1.0 / side))
                lo = t - hi * side
                left, right = [], []
                for i in range(tiles):
                    hb = jnp.broadcast_to(hi[i : i + 1], (16, LO)).astype(bf16)
                    lb = jnp.broadcast_to(lo[i : i + 1], (16, LO)).astype(bf16)
                    left.append(jnp.concatenate([jnp.where(hb == k, hs[i], zero) for k in steps], 0))
                    right.append(jnp.concatenate([jnp.where(lb == k, one, zero) for k in steps], 0))
                counts[n] += dot_nt(jnp.concatenate(left, 1), jnp.concatenate(right, 1))
        whole = (jnp.concatenate(counts, 0) * 16384.0).astype(i32)
        cut = coarse_of(jnp.concatenate([whole, jnp.zeros((3 * side, LO - side), i32)], 1), side)
        cuts = []
        for n in range(3):
            below = (cut[n * side : (n + 1) * side] <= split_bin[n]) & (iota((side, LO), 1) < side)
            below = jnp.where(below, 1.0, 0.0)
            cuts.append(jnp.sum(jnp.sum(below, axis=0, keepdims=True), axis=1, keepdims=True))
        ch_ref[n_dp] = jnp.zeros((8, row_dev), f32)
        at = iota((8, LO), 0)
        for j in range(n_dp):
            s = me ^ j
            l0, l1, l2 = [t_ref[j, n] < cuts[n] for n in range(3)]
            leaf = jnp.where(l0, jnp.where(l1, 0, 1), jnp.where(l2, 2, 3))
            g, h = t_ref[j, 3], t_ref[j, 4]
            for i in range(tiles):
                gh = jnp.where(at < 4, jnp.broadcast_to(g[i : i + 1], (8, LO)), jnp.broadcast_to(h[i : i + 1], (8, LO)))
                here = at % 4 == jnp.broadcast_to(leaf[i : i + 1], (8, LO))
                ch_ref[s, :, i * LO : (i + 1) * LO] = jnp.where(here, gh, 0.0)

    return kernel


def route_rows(blocks, slab_rows, split_bin, n_dp, row_dev):
    smem = pl.BlockSpec(memory_space=pltpu.SMEM)
    vmem = pl.BlockSpec(memory_space=pltpu.VMEM)
    return pl.pallas_call(
        make_route(n_dp, row_dev),
        out_shape=jax.ShapeDtypeStruct((n_dp + 1, 8, row_dev), f32),
        in_specs=[smem, smem] + [vmem] * len(blocks),
        out_specs=vmem,
        scratch_shapes=[pltpu.VMEM((n_dp, 5, row_dev // LO, LO), f32)],
        compiler_params=pltpu.CompilerParams(vmem_limit_bytes=32 * 2**20),
        cost_estimate=pl.CostEstimate(flops=2 * 96 * 256 * n_dp * row_dev, bytes_accessed=2**18, transcendentals=0),
        name="route",
    )(slab_rows, split_bin, *blocks)


def make_gains(n_dp, feats, row_dev):
    pairs = feats // 2
    per = row_dev // CHUNK
    width = GROUP * CHUNK

    def kernel(slab_rows, x_ref, ch_ref, o_ref, list_ref, acc_ref, cum_ref):
        def note(i, n):
            list_ref[n] = i
            return n + (i % per * CHUNK < slab_rows[i // per]).astype(i32)

        used = lax.fori_loop(0, n_dp * per, note, 0)
        for i in range(GROUP - 1):
            list_ref[used + i] = n_dp * per
        acc_ref[...] = jnp.zeros_like(acc_ref)
        kk = [to_bf16(iota((16, width), 0) // 8 + 2 * j) for j in range(HI // 2)]
        zero = jnp.zeros((16, width), bf16)
        in_first = iota((LO, LO), 1) < 64

        def add(q, _):
            xs, chs = [], []
            for i in range(GROUP):
                at = list_ref[q * GROUP + i]
                s = at // per
                col = pl.ds(pl.multiple_of((at % per) * CHUNK, CHUNK), CHUNK)
                xs.append(x_ref[jnp.minimum(s, n_dp - 1), :, col])
                chs.append(ch_ref[s, :, col])
            ch = jnp.concatenate(chs, 1)
            ch = jnp.concatenate([ch, ch], 0).astype(bf16)
            hi, lo = hi_lo(fine_of(jnp.concatenate(xs, 1)))

            def spread(f):
                hb = jnp.broadcast_to(hi[f : f + 1], (16, width)).astype(bf16)
                return [jnp.where(hb == k, ch, zero) for k in kk]

            for p in range(pairs):
                f = 2 * p
                w = jnp.concatenate(spread(f) + spread(f + 1), 0)
                a = dot_nt(hot(lo[f : f + 1], LO, width), w)
                b = dot_nt(hot(lo[f + 1 : f + 2], LO, width), w)
                acc_ref[p] += jnp.where(in_first, a, b)
            return 0

        lax.fori_loop(0, (used + GROUP - 1) // GROUP, add, 0)
        n = feats * HI
        acc = jnp.concatenate([jnp.transpose(acc_ref[p]) for p in range(pairs)], 0)
        p0 = acc.astype(bf16)
        r1 = acc - p0.astype(f32)
        p1 = r1.astype(bf16)
        r2 = r1 - p1.astype(f32)
        r, c = iota((n, n * 8), 0), iota((n, n * 8), 1)
        pick = to_bf16((c // 8 == r) & (c % 8 >= 4))
        counts = (dot_nn(pick, p0) + dot_nn(pick, p1)) + dot_nn(pick, r2.astype(bf16))
        cut = coarse_of((counts * 16384.0).astype(i32), HI).astype(f32)
        edges = [to_bf16(iota((16, LO), 0) + 16 * j) for j in range(BINS // 16)]
        one, none = jnp.ones((16, LO), bf16), jnp.zeros((16, LO), bf16)
        q0, q1 = p0.astype(f32), p1.astype(f32)
        sums = []
        for f in range(feats):
            left, right = [], []
            for k in range(HI):
                at = f * HI + k
                cb = jnp.broadcast_to(cut[at : at + 1], (16, LO)).astype(bf16)
                left.append(jnp.concatenate([jnp.where(cb <= e, one, none) for e in edges], 0))
                right.append(jnp.concatenate([q0[at * 8 : at * 8 + 8], q1[at * 8 : at * 8 + 8]], 0).astype(bf16))
            sums.append(dot_nt(jnp.concatenate(left, 1), jnp.concatenate(right, 1)))
        per_tile = LO // 16
        for f0 in range(0, feats, per_tile):
            tile = jnp.concatenate(sums[f0 : f0 + per_tile], 1)
            if tile.shape[1] < LO:
                tile = jnp.concatenate([tile, jnp.zeros((BINS, LO - tile.shape[1]), f32)], 1)
            tile = jnp.transpose(tile)
            for f in range(f0, min(f0 + per_tile, feats)):
                at = (f - f0) * 16
                gl = tile[at : at + 8] + tile[at + 8 : at + 16]
                for c in range(8):
                    cum_ref[c, f : f + 1, :] = gl[c : c + 1]

        def score(g, h):
            return g * g / (h + 1.0)

        def nodes(first):
            leaves = [cum_ref[first + c] for c in range(4)]
            a, b = leaves[0] + leaves[1], leaves[2] + leaves[3]
            return [a + b, a, b] + leaves

        for i, (gl, hl) in enumerate(zip(nodes(0), nodes(4))):
            g, h = gl[:, BINS - 1 :], hl[:, BINS - 1 :]
            o_ref[i] = score(gl, hl) + score(g - gl, h - hl) - score(g, h)

    return kernel


def gains_of(x, ch, slab_rows):
    n_dp, feats, row_dev = x.shape
    smem = pl.BlockSpec(memory_space=pltpu.SMEM)
    vmem = pl.BlockSpec(memory_space=pltpu.VMEM)
    return pl.pallas_call(
        make_gains(n_dp, feats, row_dev),
        out_shape=jax.ShapeDtypeStruct((7, feats, BINS), f32),
        in_specs=[smem, vmem, vmem],
        out_specs=vmem,
        scratch_shapes=[
            pltpu.SMEM((n_dp * (row_dev // CHUNK) + GROUP,), i32),
            pltpu.VMEM((feats // 2, LO, LO), f32),
            pltpu.VMEM((8, feats, BINS), f32),
        ],
        compiler_params=pltpu.CompilerParams(vmem_limit_bytes=40 * 2**20),
        cost_estimate=pl.CostEstimate(flops=2 * 128 * 256 * n_dp * row_dev * feats, bytes_accessed=2**20, transcendentals=0),
        name="gains",
    )(slab_rows, x, ch)


def make_pick(feat_dev, row_dev):
    tiles = row_dev // LO

    def kernel(split_feature, x_ref, o_ref, rows_ref, sems):
        me = lax.axis_index("feat")
        work = []
        for n in range(3):
            local = split_feature[n] - me * feat_dev
            owned = (local >= 0) & (local < feat_dev)
            at = jnp.clip(local, 0, feat_dev - 1)
            first = pl.multiple_of(at // 8 * 8, 8)
            copy = pltpu.make_async_copy(x_ref.at[pl.ds(first, 8), :], rows_ref.at[n], sems.at[n])
            copy.start()
            work.append((copy, at % 8, jnp.where(owned, 1.0, 0.0)))
        for n, (copy, at, scale) in enumerate(work):
            copy.wait()
            row = jnp.where(iota((8, row_dev), 0) == at, rows_ref[n], 0.0)
            row = jnp.sum(row, axis=0, keepdims=True) * scale
            for i in range(tiles):
                o_ref[n * tiles + i : n * tiles + i + 1, :] = row[:, i * LO : (i + 1) * LO]

    return kernel


def pick_rows(fine_values, split_feature):
    feat_dev, row_dev = fine_values.shape
    return pl.pallas_call(
        make_pick(feat_dev, row_dev),
        out_shape=jax.ShapeDtypeStruct((3 * row_dev // LO, LO), f32),
        in_specs=[pl.BlockSpec(memory_space=pltpu.SMEM), pl.BlockSpec(memory_space=pl.ANY)],
        out_specs=pl.BlockSpec(memory_space=pltpu.VMEM),
        scratch_shapes=[pltpu.VMEM((3, 8, row_dev), f32), pltpu.SemaphoreType.DMA((3,))],
        name="pick",
    )(split_feature, fine_values)


def swap(value, axis, size, step):
    return lax.ppermute(value, axis, [(s, s ^ step) for s in range(size)])


def make_shards(n_dp, n_feat):
    def shards(fine_values, grad, hess, slab_rows, split_feature, split_bin):
        feat_dev, row_dev = fine_values.shape
        feats = feat_dev // n_dp
        me = lax.axis_index("dp")
        both = ("dp", "feat")
        share = pick_rows(fine_values, split_feature)
        share = share + swap(share, "feat", n_feat, 1)
        gh = jnp.concatenate([grad.astype(f32).reshape(-1, LO), hess.astype(f32).reshape(-1, LO)])
        share, gh, block = lax.optimization_barrier((share, gh, jnp.concatenate([share, gh])))
        got = [swap(block, "dp", n_dp, 1)]
        for x in range(2, n_feat, 2):
            got.append(swap(share, "feat", n_feat, x))
            got.append(swap(share, both, n_dp * n_feat, n_feat + x))
        got = lax.optimization_barrier(got)
        mine, v, other_gh = share, got[0][: share.shape[0]], got[0][share.shape[0] :]
        for i in range(1, len(got), 2):
            mine, v = mine + got[i], v + got[i + 1]
        pair = jnp.stack([jnp.concatenate([mine, gh]), jnp.concatenate([v, other_gh])])
        pairs = [pair] + [swap(pair, "dp", n_dp, d) for d in range(2, n_dp, 2)]
        blocks = lax.all_to_all(fine_values.reshape(n_dp, feats, row_dev), "dp", 0, 0)
        ch = route_rows(pairs, slab_rows, split_bin, n_dp, row_dev)
        gains = gains_of(blocks, ch, slab_rows)
        pieces = [gains] + [None] * (n_dp - 1)
        for d in [*range(n_dp - 2, 0, -2), 1]:
            pieces[d] = swap(gains, "dp", n_dp, d)
        for d in range(3, n_dp, 2):
            pieces[d] = swap(pieces[d - 1], "dp", n_dp, 1)
        whole = jnp.zeros((7, feat_dev, BINS), f32)
        for d in range(n_dp):
            whole = lax.dynamic_update_slice_in_dim(whole, pieces[d], (me ^ d) * feats, 1)
        return whole

    return shards


def solution(mesh):
    return jax.shard_map(
        make_shards(mesh.shape["dp"], mesh.shape["feat"]),
        mesh=mesh,
        in_specs=(P("feat", "dp"), P("dp"), P("dp"), P(), P(), P()),
        out_specs=P(None, "feat", None),
        check_vma=False,
    )
```

```python
import jax
import jax.numpy as jnp
from jax import lax
from jax.experimental import pallas as pl
from jax.experimental.pallas import tpu as pltpu
from jax.sharding import PartitionSpec as P

FINE_BINS = 1024
BINS = 256
LO = 128
SIDE = 32
GROUP = 16
f32 = jnp.float32
bf16 = jnp.bfloat16
i32 = jnp.int32


def dot_nt(a, b):
    return lax.dot_general(a, b, (((1,), (1,)), ((), ())), preferred_element_type=f32)


def dot_nn(a, b):
    return jnp.dot(a, b, preferred_element_type=f32)


def iota(shape, axis):
    return lax.broadcasted_iota(i32, shape, axis)


def to_bf16(x):
    return x.astype(f32).astype(bf16)


def bytes_of(x, axis):
    return jnp.concatenate([to_bf16((x >> (8 * i)) & 255) for i in range(4)], axis)


def coarse_of(whole):
    n = whole.shape[0]
    r, c = iota((LO, 2 * LO), 0), iota((LO, 2 * LO), 1)
    same = r // SIDE == (c % LO) // SIDE
    in_row = dot_nn(bytes_of(whole, 0), to_bf16(same & ((r < c) | (c >= LO)))).astype(i32)
    in_row = sum(in_row[i * n : (i + 1) * n] << (8 * i) for i in range(4))
    before, row_total = in_row[:, :LO], in_row[:, LO:]
    r, c = iota((2 * n, n), 0), iota((2 * n, n), 1)
    same = (r % n) // SIDE == c // SIDE
    over = dot_nn(to_bf16(same & ((c < r) | (r >= n))), bytes_of(row_total, 1)).astype(i32)
    over = sum(over[:, i * LO : (i + 1) * LO] << (8 * i) for i in range(4))
    total = over[n:]
    remainder = before + over[:n]
    quotient = jnp.zeros_like(remainder)
    for _ in range(BINS.bit_length() - 1):
        remainder = remainder * 2
        bit = remainder >= total
        remainder = jnp.where(bit, remainder - total, remainder)
        quotient = quotient * 2 + bit.astype(i32)
    return jnp.minimum(BINS - 1, quotient)


def fine_of(v):
    return jnp.clip(jnp.floor(v * FINE_BINS), 0, FINE_BINS - 1)


def split_by(t, side):
    upper = jnp.floor(t * (1.0 / side))
    return upper, t - upper * side


def spread(rows, f):
    return jnp.broadcast_to(rows[f : f + 1], (16, rows.shape[1])).astype(bf16)


def hot(row, count, value, zero):
    at = iota(row.shape, 0)
    return [jnp.where(row == to_bf16(at + 16 * j), value, zero) for j in range(count // 16)]


def list_blocks(slab_rows, list_ref, n_dp, tiles):
    used = 0
    for s in range(n_dp):
        for i in range(tiles):
            list_ref[used + i] = s * tiles + i
        used = used + (slab_rows[s] + LO - 1) // LO
    for i in range(GROUP - 1):
        list_ref[used + i] = n_dp * tiles
    return used


def list_shape(n_dp, tiles):
    return pltpu.SMEM((n_dp * tiles + GROUP,), i32)


def params():
    return pltpu.CompilerParams(vmem_limit_bytes=40 * 2**20)


def cost(flops):
    return pl.CostEstimate(flops=flops, bytes_accessed=2**20, transcendentals=0)


def make_bins(n_dp, groups, tiles):
    blocks = n_dp * tiles
    feats = groups * 8
    quads = feats // 4
    width = GROUP * LO

    def kernel(slab_rows, x_ref, o_ref, list_ref, h_ref, cnt_ref, cut_ref, map_ref):
        used = list_blocks(slab_rows, list_ref, n_dp, tiles)
        row = iota((tiles, LO), 0) * LO + iota((tiles, LO), 1)
        for s in range(n_dp):
            h = jnp.where(row < slab_rows[s], x_ref[s, groups * tiles + 1], 0.0)
            for i in range(tiles):
                h_ref[s * tiles + i] = jnp.broadcast_to(h[i : i + 1], (8, LO))
        h_ref[blocks] = jnp.zeros((8, LO), f32)
        cnt_ref[...] = jnp.zeros_like(cnt_ref)
        one, zero = jnp.ones((16, width), bf16), jnp.zeros((16, width), bf16)

        def fine_block(at):
            s, i = jnp.minimum(at // tiles, n_dp - 1), at % tiles
            return fine_of(jnp.concatenate([x_ref[s, g * tiles + i] for g in range(groups)], 0))

        def count(q, _):
            ts, hs = [], []
            for i in range(GROUP):
                at = list_ref[q * GROUP + i]
                ts.append(fine_block(at))
                hs.append(h_ref[at])
            h = jnp.concatenate(hs, 1)
            h = jnp.concatenate([h, h], 0).astype(bf16)
            upper, lower = split_by(jnp.concatenate(ts, 1), SIDE)
            for quad in range(quads):
                left, right = [], []
                for f in range(quad * 4, quad * 4 + 4):
                    left += hot(spread(upper, f), SIDE, h, zero)
                    right += hot(spread(lower, f), SIDE, one, zero)
                cnt_ref[quad] += dot_nt(jnp.concatenate(left, 0), jnp.concatenate(right, 0))
            return 0

        rounds = (used + GROUP - 1) // GROUP
        lax.fori_loop(0, rounds, count, 0)
        counts = []
        for quad in range(quads):
            lane = iota((SIDE, LO), 1) // SIDE
            mine = cnt_ref[quad, :SIDE]
            for i in range(1, 4):
                mine = jnp.where(lane == i, cnt_ref[quad, i * SIDE : (i + 1) * SIDE], mine)
            counts.append(mine)
        counts = jnp.concatenate(counts, 0)
        cut_ref[...] = coarse_of((counts * 16384.0).astype(i32)).astype(f32)
        lane = iota((quads * 8, LO), 1) // SIDE
        sub = iota((8, LO), 0)
        rows = [cut_ref[pl.ds(i, quads * 8, 4), :] for i in range(4)]
        words = [jnp.zeros((8, LO), i32) for _ in range(quads)]
        for q in range(4):
            table = jnp.zeros((quads * 8, LO), f32)
            for i in range(4):
                shift = (i - q) * SIDE % LO
                moved = pltpu.roll(rows[i], shift, 1) if shift else rows[i]
                table = jnp.where(lane == i, moved, table)
            for quad in range(quads):
                word = table[quad * 8 : quad * 8 + 8].astype(i32) << (sub % 4 * 8)
                word = word + pltpu.roll(word, 7, 0)
                word = word + pltpu.roll(word, 6, 0)
                word = pltpu.roll(word, q, 0) if q else word
                words[quad] = jnp.where(sub % 4 == q, word, words[quad])
        for quad in range(quads):
            map_ref[quad] = words[quad]
        upper_half = sub >= 4

        def look_up(q, _):
            for i in range(GROUP):
                at = list_ref[q * GROUP + i]
                fine = fine_block(at).astype(i32)
                for g in range(groups):
                    here = fine[g * 8 : g * 8 + 8]
                    turned = pltpu.roll(here, 4, 0)
                    found = []
                    for half in range(2):
                        t = jnp.where(upper_half, turned, here) if half == 0 else jnp.where(upper_half, here, turned)
                        word = jnp.take_along_axis(map_ref[g * 2 + half], t & (LO - 1), axis=1, mode="promise_in_bounds")
                        value = (word >> ((t >> 4) & 24)) & 255
                        value = jnp.where((t >= FINE_BINS // 2) == upper_half, value, 0)
                        found.append(value + pltpu.roll(value, 4, 0))
                    o_ref[at, g * 8 : g * 8 + 8, :] = jnp.where(upper_half, found[1], found[0]).astype(f32)
            return 0

        lax.fori_loop(0, rounds, look_up, 0)

    return kernel


def find_bins(x, slab_rows, groups, tiles):
    n_dp = x.shape[0]
    feats = groups * 8
    smem = pl.BlockSpec(memory_space=pltpu.SMEM)
    vmem = pl.BlockSpec(memory_space=pltpu.VMEM)
    return pl.pallas_call(
        make_bins(n_dp, groups, tiles),
        out_shape=jax.ShapeDtypeStruct((n_dp * tiles + 1, feats, LO), f32),
        in_specs=[smem, vmem],
        out_specs=vmem,
        scratch_shapes=[
            list_shape(n_dp, tiles),
            pltpu.VMEM((n_dp * tiles + 1, 8, LO), f32),
            pltpu.VMEM((feats // 4, LO, LO), f32),
            pltpu.VMEM((feats // 4 * SIDE, LO), f32),
            pltpu.VMEM((feats // 4, 8, LO), i32),
        ],
        compiler_params=params(),
        cost_estimate=cost(2 * 128 * 128 * n_dp * tiles * LO * feats // 4),
        name="bins",
    )(slab_rows, x)


def make_route(n_dp, groups, tiles):
    blocks = n_dp * tiles

    def kernel(slab_rows, split_bin, x_ref, *refs):
        pairs, ch_ref, t_ref = refs[: n_dp // 2], refs[n_dp // 2], refs[n_dp // 2 + 1]
        me = lax.axis_index("dp")
        one, zero = jnp.ones((16, LO), bf16), jnp.zeros((16, LO), bf16)
        counts = jnp.zeros((LO, LO), f32)
        nothing = [zero] * (SIDE // 16)
        for j in range(n_dp):
            s = me ^ j
            row = iota((tiles, LO), 0) * LO + iota((tiles, LO), 1)
            live = row < slab_rows[s]
            t_ref[j, 3] = jnp.where(live, x_ref[s, groups * tiles], 0.0)
            h = jnp.where(live, x_ref[s, groups * tiles + 1], 0.0)
            t_ref[j, 4] = h
            lefts, rights = [], []
            hs = [spread(h, i) for i in range(tiles)]
            for n in range(3):
                t = fine_of(pairs[j // 2][j % 2, n * tiles : (n + 1) * tiles])
                t_ref[j, n] = t
                upper, lower = split_by(t, SIDE)
                left = [jnp.concatenate(hot(spread(upper, i), SIDE, hs[i], zero), 0) for i in range(tiles)]
                right = [jnp.concatenate(hot(spread(lower, i), SIDE, one, zero), 0) for i in range(tiles)]
                lefts.append(jnp.concatenate(left, 1))
                rights.append(jnp.concatenate(right, 1))
            empty = jnp.zeros((SIDE, tiles * LO), bf16)
            counts += dot_nt(jnp.concatenate(lefts + [empty], 0), jnp.concatenate(rights + [empty], 0))
        lane = iota((SIDE, LO), 1)
        mine = counts[:SIDE]
        for n in range(1, 3):
            mine = jnp.where(lane // SIDE == n, counts[n * SIDE : (n + 1) * SIDE], mine)
        mine = jnp.where(lane < 3 * SIDE, (mine * 16384.0).astype(i32), 1)
        cut = coarse_of(mine)
        bound = jnp.where(lane < SIDE, split_bin[0], jnp.where(lane < 2 * SIDE, split_bin[1], split_bin[2]))
        below = jnp.sum(jnp.where(cut <= bound, 1.0, 0.0), axis=0, keepdims=True)
        lane = lane[:1]
        cuts = [jnp.sum(jnp.where(lane // SIDE == n, below, 0.0), axis=1, keepdims=True) for n in range(3)]
        ch_ref[blocks] = jnp.zeros((8, LO), f32)
        at = iota((8, LO), 0)
        for j in range(n_dp):
            s = me ^ j
            l0, l1, l2 = [t_ref[j, n] < cuts[n] for n in range(3)]
            leaf = jnp.where(l0, jnp.where(l1, 0, 1), jnp.where(l2, 2, 3))
            g, h = t_ref[j, 3], t_ref[j, 4]
            for i in range(tiles):
                gh = jnp.where(at < 4, jnp.broadcast_to(g[i : i + 1], (8, LO)), jnp.broadcast_to(h[i : i + 1], (8, LO)))
                here = at % 4 == jnp.broadcast_to(leaf[i : i + 1], (8, LO))
                ch_ref[s * tiles + i] = jnp.where(here, gh, 0.0)

    return kernel


def make_gains(n_dp, feats_all, feats, tiles):
    quads = feats_all // 4
    width = GROUP * LO
    inner = 64

    def kernel(slab_rows, bin_ref, ch_ref, o_ref, list_ref, acc_ref, cum_ref):
        used = list_blocks(slab_rows, list_ref, n_dp, tiles)
        acc_ref[...] = jnp.zeros_like(acc_ref)
        kk = [to_bf16(iota((16, width), 0) // 8 + 2 * j) for j in range(2)]
        one, zero = jnp.ones((16, width), bf16), jnp.zeros((16, width), bf16)
        lane = iota((inner, LO), 1) // SIDE

        def add(q, _):
            bs, chs = [], []
            for i in range(GROUP):
                at = list_ref[q * GROUP + i]
                bs.append(bin_ref[at])
                chs.append(ch_ref[at])
            ch = jnp.concatenate(chs, 1)
            ch = jnp.concatenate([ch, ch], 0).astype(bf16)
            upper, lower = split_by(jnp.concatenate(bs, 1), inner)
            for quad in range(quads):
                left, right = [], []
                for f in range(quad * 4, quad * 4 + 4):
                    left += hot(spread(lower, f), inner, one, zero)
                    u = spread(upper, f)
                    right += [jnp.where(u == k, ch, zero) for k in kk]
                out = dot_nt(jnp.concatenate(left, 0), jnp.concatenate(right, 0))
                mine = out[:inner]
                for i in range(1, 4):
                    mine = jnp.where(lane == i, out[i * inner : (i + 1) * inner], mine)
                acc_ref[quad] += mine
            return 0

        lax.fori_loop(0, (used + GROUP - 1) // GROUP, add, 0)
        r, c = iota((inner, LO), 0), iota((inner, LO), 1)
        upto = to_bf16((r <= c) | (c >= inner))
        pad = jnp.zeros((LO - inner, LO), f32)
        for quad in range(quads):
            acc = jnp.transpose(jnp.concatenate([acc_ref[quad], pad], 0))[:, :inner]
            p0 = acc.astype(bf16)
            r1 = acc - p0.astype(f32)
            p1 = r1.astype(bf16)
            p2 = (r1 - p1.astype(f32)).astype(bf16)
            run = (dot_nn(p0, upto) + dot_nn(p1, upto)) + dot_nn(p2, upto)
            whole = pltpu.roll(run, inner, 1)
            first = iota((8, LO), 1) < inner
            for i in range(4):
                f = quad * 4 + i
                if f >= feats:
                    break
                base = jnp.zeros((8, LO), f32)
                for k in range(0, 4, 2):
                    a = (i * 4 + k) * 8
                    ta = jnp.where(first, whole[a : a + 8], run[a : a + 8])
                    tb = jnp.where(first, whole[a + 8 : a + 16], run[a + 8 : a + 16])
                    gl = base + jnp.where(first, run[a : a + 8], ta + whole[a + 8 : a + 16])
                    base = base + (ta + tb)
                    for c in range(8):
                        cum_ref[c, f : f + 1, k // 2 * LO : k // 2 * LO + LO] = gl[c : c + 1]

        def score(g, h):
            return g * g / (h + 1.0)

        def nodes(at):
            leaves = [cum_ref[at + c] for c in range(4)]
            a, b = leaves[0] + leaves[1], leaves[2] + leaves[3]
            return [a + b, a, b] + leaves

        for i, (gl, hl) in enumerate(zip(nodes(0), nodes(4))):
            g, h = gl[:, BINS - 1 :], hl[:, BINS - 1 :]
            o_ref[i] = score(gl, hl) + score(g - gl, h - hl) - score(g, h)

    return kernel


def route_and_sum(x, pairs, bins, slab_rows, split_bin, feats, groups, tiles):
    n_dp = x.shape[0]
    blocks, feats_all = n_dp * tiles, groups * 8
    smem = pl.BlockSpec(memory_space=pltpu.SMEM)
    vmem = pl.BlockSpec(memory_space=pltpu.VMEM)
    route = make_route(n_dp, groups, tiles)
    sum_up = make_gains(n_dp, feats_all, feats, tiles)

    def kernel(slab_rows, split_bin, x_ref, bin_ref, *refs):
        o_ref, list_ref, ch_ref, t_ref, acc_ref, cum_ref = refs[n_dp // 2 :]
        route(slab_rows, split_bin, x_ref, *refs[: n_dp // 2], ch_ref, t_ref)
        sum_up(slab_rows, bin_ref, ch_ref, o_ref, list_ref, acc_ref, cum_ref)

    return pl.pallas_call(
        kernel,
        out_shape=jax.ShapeDtypeStruct((7, feats, BINS), f32),
        in_specs=[smem, smem] + [vmem] * (2 + len(pairs)),
        out_specs=vmem,
        scratch_shapes=[
            list_shape(n_dp, tiles),
            pltpu.VMEM((blocks + 1, 8, LO), f32),
            pltpu.VMEM((n_dp, 5, tiles, LO), f32),
            pltpu.VMEM((feats_all // 4, 64, LO), f32),
            pltpu.VMEM((8, feats, BINS), f32),
        ],
        compiler_params=params(),
        cost_estimate=cost(2 * 128 * 256 * blocks * LO * feats_all // 4),
        name="gains",
    )(slab_rows, split_bin, x, bins, *pairs)


def make_pick(groups, tiles, feat_dev, feats):
    def kernel(split_feature, x_ref, g_ref, h_ref, o_ref, x_out, sems):
        me = lax.axis_index("feat")
        n_dp = x_ref.shape[0]
        size = groups * tiles
        copies = [pltpu.make_async_copy(x_ref.at[s], x_out.at[s, pl.ds(0, size)], sems.at[s]) for s in range(n_dp)]
        for copy in copies:
            copy.start()
        g, h = g_ref[...].astype(f32), h_ref[...].astype(f32)
        for s in range(n_dp):
            x_out[s, size] = g
            x_out[s, size + 1] = h
        for copy in copies:
            copy.wait()
        at8 = iota((8, LO), 0)
        for n in range(3):
            local = split_feature[n] - me * feat_dev
            owned = (local >= 0) & (local < feat_dev)
            at = jnp.clip(local, 0, feat_dev - 1)
            s, f = at // feats, at % feats
            mine = (at8 == f % 8) & owned
            for i in range(tiles):
                tile = x_out[s, f // 8 * tiles + i]
                o_ref[n * tiles + i : n * tiles + i + 1, :] = jnp.sum(jnp.where(mine, tile, 0.0), axis=0, keepdims=True)

    return kernel


def pick_rows(x, grad, hess, split_feature, groups, tiles, feat_dev):
    n_dp = x.shape[0]
    smem = pl.BlockSpec(memory_space=pltpu.SMEM)
    vmem = pl.BlockSpec(memory_space=pltpu.VMEM)
    return pl.pallas_call(
        make_pick(groups, tiles, feat_dev, feat_dev // n_dp),
        out_shape=[
            jax.ShapeDtypeStruct((3 * tiles, LO), f32),
            jax.ShapeDtypeStruct((n_dp, groups * tiles + 2, 8, LO), f32),
        ],
        in_specs=[smem, pl.BlockSpec(memory_space=pl.ANY), vmem, vmem],
        out_specs=[vmem, vmem],
        scratch_shapes=[pltpu.SemaphoreType.DMA((n_dp,))],
        name="pick",
    )(split_feature, x, grad.reshape(tiles, LO), hess.reshape(tiles, LO))


def swap(value, axis, size, step):
    return lax.ppermute(value, axis, [(s, s ^ step) for s in range(size)])


def make_shards(n_dp, n_feat):
    def shards(fine_values, grad, hess, slab_rows, split_feature, split_bin):
        feat_dev, row_dev = fine_values.shape
        feats, tiles = feat_dev // n_dp, row_dev // LO
        groups = (feats + 7) // 8
        me = lax.axis_index("dp")
        both = ("dp", "feat")
        x = fine_values.reshape(n_dp, feats, tiles, LO)
        x = jnp.pad(x, ((0, 0), (0, groups * 8 - feats), (0, 0), (0, 0)))
        x = x.reshape(n_dp, groups, 8, tiles, LO).swapaxes(2, 3).reshape(n_dp, groups * tiles, 8, LO)
        share, x = pick_rows(x, grad, hess, split_feature, groups, tiles, feat_dev)
        share = share + swap(share, "feat", n_feat, 1)
        got = [swap(share, "dp", n_dp, 1)]
        for i in range(2, n_feat, 2):
            got.append(swap(share, "feat", n_feat, i))
            got.append(swap(share, both, n_dp * n_feat, n_feat + i))
        got = lax.optimization_barrier(got)
        mine, other = share, got[0]
        for i in range(1, len(got), 2):
            mine, other = mine + got[i], other + got[i + 1]
        pair = jnp.stack([mine, other])
        pairs = [pair] + [swap(pair, "dp", n_dp, d) for d in range(2, n_dp, 2)]
        x = lax.all_to_all(x, "dp", 0, 0)
        bins = find_bins(x, slab_rows, groups, tiles)
        gains = route_and_sum(x, pairs, bins, slab_rows, split_bin, feats, groups, tiles)
        pieces = [gains] + [None] * (n_dp - 1)
        for d in [*range(n_dp - 2, 0, -2), 1]:
            pieces[d] = swap(gains, "dp", n_dp, d)
        for d in range(3, n_dp, 2):
            pieces[d] = swap(pieces[d - 1], "dp", n_dp, 1)
        whole = jnp.zeros((7, feat_dev, BINS), f32)
        order = [4, 2, 1] + [*range(6, n_dp, 2)] + [*range(3, n_dp, 2)]
        for d in [0] + [d for d in order if d < n_dp]:
            whole = lax.dynamic_update_slice_in_dim(whole, pieces[d], (me ^ d) * feats, 1)
        return whole

    return shards


def solution(mesh):
    return jax.shard_map(
        make_shards(mesh.shape["dp"], mesh.shape["feat"]),
        mesh=mesh,
        in_specs=(P("feat", "dp"), P("dp"), P("dp"), P(), P(), P()),
        out_specs=P(None, "feat", None),
        check_vma=False,
    )
```

```python
import jax
import jax.numpy as jnp
from jax import lax
from jax.experimental import pallas as pl
from jax.experimental.pallas import tpu as pltpu
from jax.sharding import PartitionSpec as P

FINE_BINS = 1024
BINS = 256
LO = 128
SIDE = 32
UPPER = 6
INNER = 48
GROUP = 16
f32 = jnp.float32
bf16 = jnp.bfloat16
i32 = jnp.int32


def dot_nt(a, b):
    return lax.dot_general(a, b, (((1,), (1,)), ((), ())), preferred_element_type=f32)


def dot_nn(a, b):
    return jnp.dot(a, b, preferred_element_type=f32)


def iota(shape, axis):
    return lax.broadcasted_iota(i32, shape, axis)


def to_bf16(x):
    return x.astype(f32).astype(bf16)


def bytes_of(x, axis):
    return jnp.concatenate([to_bf16((x >> (8 * i)) & 255) for i in range(4)], axis)


def coarse_of(whole):
    n = whole.shape[0]
    r, c = iota((LO, 2 * LO), 0), iota((LO, 2 * LO), 1)
    same = r // SIDE == (c % LO) // SIDE
    in_row = dot_nn(bytes_of(whole, 0), to_bf16(same & ((r < c) | (c >= LO)))).astype(i32)
    in_row = sum(in_row[i * n : (i + 1) * n] << (8 * i) for i in range(4))
    before, row_total = in_row[:, :LO], in_row[:, LO:]
    r, c = iota((2 * n, n), 0), iota((2 * n, n), 1)
    same = (r % n) // SIDE == c // SIDE
    over = dot_nn(to_bf16(same & ((c < r) | (r >= n))), bytes_of(row_total, 1)).astype(i32)
    over = sum(over[:, i * LO : (i + 1) * LO] << (8 * i) for i in range(4))
    total = over[n:]
    remainder = before + over[:n]
    quotient = jnp.zeros_like(remainder)
    for _ in range(BINS.bit_length() - 1):
        remainder = remainder * 2
        bit = remainder >= total
        remainder = jnp.where(bit, remainder - total, remainder)
        quotient = quotient * 2 + bit.astype(i32)
    return jnp.minimum(BINS - 1, quotient)


def fine_of(v):
    return jnp.clip(jnp.floor(v * FINE_BINS), 0, FINE_BINS - 1)


def split_by(t, side):
    upper = jnp.floor(t * (1.0 / side))
    return upper, t - upper * side


def spread(rows, f):
    return jnp.broadcast_to(rows[f : f + 1], (16, rows.shape[1])).astype(bf16)


def hot(row, count, value, zero):
    at = iota(row.shape, 0)
    return [jnp.where(row == to_bf16(at + 16 * j), value, zero) for j in range(count // 16)]


def list_blocks(slab_rows, list_ref, n_dp, tiles):
    used = 0
    for s in range(n_dp):
        for i in range(tiles):
            list_ref[used + i] = s * tiles + i
        used = used + (slab_rows[s] + LO - 1) // LO
    for i in range(GROUP - 1):
        list_ref[used + i] = n_dp * tiles
    return used


def list_shape(n_dp, tiles):
    return pltpu.SMEM((n_dp * tiles + GROUP,), i32)


def params():
    return pltpu.CompilerParams(vmem_limit_bytes=40 * 2**20)


def cost(flops):
    return pl.CostEstimate(flops=flops, bytes_accessed=2**20, transcendentals=0)


def make_bins(n_dp, groups, tiles):
    blocks = n_dp * tiles
    feats = groups * 8
    quads = feats // 4
    width = GROUP * LO

    def kernel(slab_rows, x_ref, o_ref, list_ref, h_ref, cnt_ref, cut_ref, map_ref):
        used = list_blocks(slab_rows, list_ref, n_dp, tiles)
        row = iota((tiles, LO), 0) * LO + iota((tiles, LO), 1)
        for s in range(n_dp):
            h = jnp.where(row < slab_rows[s], x_ref[s, groups * tiles], 0.0)
            for i in range(tiles):
                h_ref[s * tiles + i] = jnp.broadcast_to(h[i : i + 1], (8, LO))
        h_ref[blocks] = jnp.zeros((8, LO), f32)
        cnt_ref[...] = jnp.zeros_like(cnt_ref)
        one, zero = jnp.ones((16, width), bf16), jnp.zeros((16, width), bf16)

        def fine_block(at):
            s, i = jnp.minimum(at // tiles, n_dp - 1), at % tiles
            return fine_of(jnp.concatenate([x_ref[s, g * tiles + i] for g in range(groups)], 0))

        def count(q, _):
            ts, hs = [], []
            for i in range(GROUP):
                at = list_ref[q * GROUP + i]
                ts.append(fine_block(at))
                hs.append(h_ref[at])
            h = jnp.concatenate(hs, 1)
            h = jnp.concatenate([h, h], 0).astype(bf16)
            upper, lower = split_by(jnp.concatenate(ts, 1), SIDE)
            for quad in range(quads):
                left, right = [], []
                for f in range(quad * 4, quad * 4 + 4):
                    left += hot(spread(upper, f), SIDE, h, zero)
                    right += hot(spread(lower, f), SIDE, one, zero)
                cnt_ref[quad] += dot_nt(jnp.concatenate(left, 0), jnp.concatenate(right, 0))
            return 0

        rounds = (used + GROUP - 1) // GROUP
        lax.fori_loop(0, rounds, count, 0)
        counts = []
        for quad in range(quads):
            lane = iota((SIDE, LO), 1) // SIDE
            mine = cnt_ref[quad, :SIDE]
            for i in range(1, 4):
                mine = jnp.where(lane == i, cnt_ref[quad, i * SIDE : (i + 1) * SIDE], mine)
            counts.append(mine)
        counts = jnp.concatenate(counts, 0)
        cut_ref[...] = coarse_of((counts * 16384.0).astype(i32)).astype(f32)
        lane = iota((quads * 8, LO), 1) // SIDE
        sub = iota((8, LO), 0)
        rows = [cut_ref[pl.ds(i, quads * 8, 4), :] for i in range(4)]
        words = [jnp.zeros((8, LO), i32) for _ in range(quads)]
        for q in range(4):
            table = jnp.zeros((quads * 8, LO), f32)
            for i in range(4):
                shift = (i - q) * SIDE % LO
                moved = pltpu.roll(rows[i], shift, 1) if shift else rows[i]
                table = jnp.where(lane == i, moved, table)
            for quad in range(quads):
                word = table[quad * 8 : quad * 8 + 8].astype(i32) << (sub % 4 * 8)
                word = word + pltpu.roll(word, 7, 0)
                word = word + pltpu.roll(word, 6, 0)
                word = pltpu.roll(word, q, 0) if q else word
                words[quad] = jnp.where(sub % 4 == q, word, words[quad])
        for quad in range(quads):
            map_ref[quad] = words[quad]
        upper_half = sub >= 4

        def look_up(q, _):
            for i in range(GROUP):
                at = list_ref[q * GROUP + i]
                fine = fine_block(at).astype(i32)
                for g in range(groups):
                    here = fine[g * 8 : g * 8 + 8]
                    turned = pltpu.roll(here, 4, 0)
                    found = []
                    for half in range(2):
                        t = jnp.where(upper_half, turned, here) if half == 0 else jnp.where(upper_half, here, turned)
                        word = jnp.take_along_axis(map_ref[g * 2 + half], t & (LO - 1), axis=1, mode="promise_in_bounds")
                        value = (word >> ((t >> 4) & 24)) & 255
                        value = jnp.where((t >= FINE_BINS // 2) == upper_half, value, 0)
                        found.append(value + pltpu.roll(value, 4, 0))
                    o_ref[at, g * 8 : g * 8 + 8, :] = jnp.where(upper_half, found[1], found[0]).astype(f32)
            return 0

        lax.fori_loop(0, rounds, look_up, 0)

    return kernel


def find_bins(x, slab_rows, groups, tiles):
    n_dp = x.shape[0]
    feats = groups * 8
    smem = pl.BlockSpec(memory_space=pltpu.SMEM)
    vmem = pl.BlockSpec(memory_space=pltpu.VMEM)
    return pl.pallas_call(
        make_bins(n_dp, groups, tiles),
        out_shape=jax.ShapeDtypeStruct((n_dp * tiles + 1, feats, LO), f32),
        in_specs=[smem, vmem],
        out_specs=vmem,
        scratch_shapes=[
            list_shape(n_dp, tiles),
            pltpu.VMEM((n_dp * tiles + 1, 8, LO), f32),
            pltpu.VMEM((feats // 4, LO, LO), f32),
            pltpu.VMEM((feats // 4 * SIDE, LO), f32),
            pltpu.VMEM((feats // 4, 8, LO), i32),
        ],
        compiler_params=params(),
        cost_estimate=cost(2 * 128 * 128 * n_dp * tiles * LO * feats // 4),
        name="bins",
    )(slab_rows, x)


def make_route(n_dp, groups, tiles):
    blocks = n_dp * tiles

    def kernel(slab_rows, split_bin, x_ref, *refs):
        pairs, ch_ref, t_ref = refs[: n_dp // 2], refs[n_dp // 2], refs[n_dp // 2 + 1]
        me = lax.axis_index("dp")
        one, zero = jnp.ones((16, LO), bf16), jnp.zeros((16, LO), bf16)
        counts = jnp.zeros((LO, LO), f32)
        nothing = [zero] * (SIDE // 16)
        for j in range(n_dp):
            s = me ^ j
            row = iota((tiles, LO), 0) * LO + iota((tiles, LO), 1)
            live = row < slab_rows[s]
            t_ref[j, 3] = jnp.where(live, pairs[j // 2][j % 2, 3 * tiles :], 0.0)
            h = jnp.where(live, x_ref[s, groups * tiles], 0.0)
            t_ref[j, 4] = h
            lefts, rights = [], []
            hs = [spread(h, i) for i in range(tiles)]
            for n in range(3):
                t = fine_of(pairs[j // 2][j % 2, n * tiles : (n + 1) * tiles])
                t_ref[j, n] = t
                upper, lower = split_by(t, SIDE)
                left = [jnp.concatenate(hot(spread(upper, i), SIDE, hs[i], zero), 0) for i in range(tiles)]
                right = [jnp.concatenate(hot(spread(lower, i), SIDE, one, zero), 0) for i in range(tiles)]
                lefts.append(jnp.concatenate(left, 1))
                rights.append(jnp.concatenate(right, 1))
            empty = jnp.zeros((SIDE, tiles * LO), bf16)
            counts += dot_nt(jnp.concatenate(lefts + [empty], 0), jnp.concatenate(rights + [empty], 0))
        lane = iota((SIDE, LO), 1)
        mine = counts[:SIDE]
        for n in range(1, 3):
            mine = jnp.where(lane // SIDE == n, counts[n * SIDE : (n + 1) * SIDE], mine)
        mine = jnp.where(lane < 3 * SIDE, (mine * 16384.0).astype(i32), 1)
        cut = coarse_of(mine)
        bound = jnp.where(lane < SIDE, split_bin[0], jnp.where(lane < 2 * SIDE, split_bin[1], split_bin[2]))
        below = jnp.sum(jnp.where(cut <= bound, 1.0, 0.0), axis=0, keepdims=True)
        lane = lane[:1]
        cuts = [jnp.sum(jnp.where(lane // SIDE == n, below, 0.0), axis=1, keepdims=True) for n in range(3)]
        ch_ref[blocks] = jnp.zeros((8, LO), f32)
        at = iota((8, LO), 0)
        for j in range(n_dp):
            s = me ^ j
            l0, l1, l2 = [t_ref[j, n] < cuts[n] for n in range(3)]
            leaf = jnp.where(l0, jnp.where(l1, 0, 1), jnp.where(l2, 2, 3))
            g, h = t_ref[j, 3], t_ref[j, 4]
            for i in range(tiles):
                gh = jnp.where(at < 4, jnp.broadcast_to(g[i : i + 1], (8, LO)), jnp.broadcast_to(h[i : i + 1], (8, LO)))
                here = at % 4 == jnp.broadcast_to(leaf[i : i + 1], (8, LO))
                ch_ref[s * tiles + i] = jnp.where(here, gh, 0.0)

    return kernel


def make_gains(n_dp, feats_all, feats, tiles):
    quads = feats_all // 4
    width = GROUP * LO
    lanes = 4 * UPPER * 8

    def kernel(slab_rows, bin_ref, ch_ref, o_ref, list_ref, acc_ref, cum_ref):
        used = list_blocks(slab_rows, list_ref, n_dp, tiles)
        acc_ref[...] = jnp.zeros_like(acc_ref)
        kk = [to_bf16(iota((16, width), 0) // 8 + 2 * j) for j in range(UPPER // 2)]
        one, zero = jnp.ones((16, width), bf16), jnp.zeros((16, width), bf16)
        lane = iota((INNER, lanes), 1) // (UPPER * 8)

        def add(q, _):
            bs, chs = [], []
            for i in range(GROUP):
                at = list_ref[q * GROUP + i]
                bs.append(bin_ref[at])
                chs.append(ch_ref[at])
            ch = jnp.concatenate(chs, 1)
            ch = jnp.concatenate([ch, ch], 0).astype(bf16)
            bins = jnp.concatenate(bs, 1)
            upper = jnp.floor((bins + 0.5) * (1.0 / INNER))
            lower = bins - upper * INNER
            for quad in range(quads):
                left, right = [], []
                for f in range(quad * 4, quad * 4 + 4):
                    left += hot(spread(lower, f), INNER, one, zero)
                    u = spread(upper, f)
                    right += [jnp.where(u == k, ch, zero) for k in kk]
                out = dot_nt(jnp.concatenate(left, 0), jnp.concatenate(right, 0))
                mine = out[:INNER]
                for i in range(1, 4):
                    mine = jnp.where(lane == i, out[i * INNER : (i + 1) * INNER], mine)
                acc_ref[quad, :INNER, :lanes] += mine
            return 0

        lax.fori_loop(0, (used + GROUP - 1) // GROUP, add, 0)
        r, c = iota((LO, 2 * LO), 0), iota((LO, 2 * LO), 1)
        upto = to_bf16(r <= c)
        at = iota((8, LO), 1)
        for quad in range(quads):
            acc = jnp.concatenate([jnp.transpose(acc_ref[quad, :, :LO]), jnp.transpose(acc_ref[quad, :, LO:])], 0)[:lanes]
            p0 = acc.astype(bf16)
            r1 = acc - p0.astype(f32)
            p1 = r1.astype(bf16)
            p2 = (r1 - p1.astype(f32)).astype(bf16)
            run = (dot_nn(p0, upto) + dot_nn(p1, upto)) + dot_nn(p2, upto)
            for i in range(4):
                f = quad * 4 + i
                if f >= feats:
                    break
                for t in range(BINS // LO):
                    gl = jnp.zeros((8, LO), f32)
                    for k in range(UPPER):
                        row = (i * UPPER + k) * 8
                        part, total = run[row : row + 8, :LO], run[row : row + 8, LO:]
                        s = INNER * k - LO * t
                        if s >= LO:
                            continue
                        if s <= -INNER:
                            part = total
                        elif s < 0:
                            part = jnp.where(at < LO + s, pltpu.roll(part, LO + s, 1), total)
                        elif s > 0:
                            part = jnp.where(at >= s, pltpu.roll(part, s, 1), 0.0)
                        gl = gl + part
                    for c in range(8):
                        cum_ref[c, f : f + 1, t * LO : t * LO + LO] = gl[c : c + 1]

        def score(g, h):
            return g * g / (h + 1.0)

        def nodes(at):
            leaves = [cum_ref[at + c] for c in range(4)]
            a, b = leaves[0] + leaves[1], leaves[2] + leaves[3]
            return [a + b, a, b] + leaves

        for i, (gl, hl) in enumerate(zip(nodes(0), nodes(4))):
            g, h = gl[:, BINS - 1 :], hl[:, BINS - 1 :]
            o_ref[i] = score(gl, hl) + score(g - gl, h - hl) - score(g, h)

    return kernel


def route_and_sum(x, pairs, bins, slab_rows, split_bin, feats, groups, tiles):
    n_dp = x.shape[0]
    blocks, feats_all = n_dp * tiles, groups * 8
    smem = pl.BlockSpec(memory_space=pltpu.SMEM)
    vmem = pl.BlockSpec(memory_space=pltpu.VMEM)
    route = make_route(n_dp, groups, tiles)
    sum_up = make_gains(n_dp, feats_all, feats, tiles)

    def kernel(slab_rows, split_bin, x_ref, bin_ref, *refs):
        o_ref, list_ref, ch_ref, t_ref, acc_ref, cum_ref = refs[n_dp // 2 :]
        route(slab_rows, split_bin, x_ref, *refs[: n_dp // 2], ch_ref, t_ref)
        sum_up(slab_rows, bin_ref, ch_ref, o_ref, list_ref, acc_ref, cum_ref)

    return pl.pallas_call(
        kernel,
        out_shape=jax.ShapeDtypeStruct((7, feats, BINS), f32),
        in_specs=[smem, smem] + [vmem] * (2 + len(pairs)),
        out_specs=vmem,
        scratch_shapes=[
            list_shape(n_dp, tiles),
            pltpu.VMEM((blocks + 1, 8, LO), f32),
            pltpu.VMEM((n_dp, 5, tiles, LO), f32),
            pltpu.VMEM((feats_all // 4, LO, 2 * LO), f32),
            pltpu.VMEM((8, feats, BINS), f32),
        ],
        compiler_params=params(),
        cost_estimate=cost(2 * 128 * 256 * blocks * LO * feats_all // 4),
        name="gains",
    )(slab_rows, split_bin, x, bins, *pairs)


def make_pick(groups, tiles, feat_dev, feats):
    def kernel(split_ref, x_ref, h_ref, o_ref, x_out, split_feature, h_in, sems):
        me = lax.axis_index("feat")
        n_dp = x_ref.shape[0]
        size = groups * tiles
        split_copy = pltpu.make_async_copy(split_ref, split_feature, sems.at[n_dp + 1])
        split_copy.start()
        h_copy = pltpu.make_async_copy(h_ref, h_in, sems.at[n_dp])
        h_copy.start()
        copies = [pltpu.make_async_copy(x_ref.at[s], x_out.at[s, pl.ds(0, size)], sems.at[s]) for s in range(n_dp)]
        for copy in copies:
            copy.start()
        h_copy.wait()
        h = h_in[...].astype(f32)
        for s in range(n_dp):
            x_out[s, size] = h
        split_copy.wait()
        for copy in copies:
            copy.wait()
        at8 = iota((8, LO), 0)
        for n in range(3):
            local = split_feature[n] - me * feat_dev
            owned = (local >= 0) & (local < feat_dev)
            at = jnp.clip(local, 0, feat_dev - 1)
            s, f = at // feats, at % feats
            mine = (at8 == f % 8) & owned
            for i in range(tiles):
                tile = x_out[s, f // 8 * tiles + i]
                o_ref[n * tiles + i : n * tiles + i + 1, :] = jnp.sum(jnp.where(mine, tile, 0.0), axis=0, keepdims=True)

    return kernel


def pick_rows(x, hess, split_feature, groups, tiles, feat_dev):
    n_dp = x.shape[0]
    anywhere = pl.BlockSpec(memory_space=pl.ANY)
    vmem = pl.BlockSpec(memory_space=pltpu.VMEM)
    return pl.pallas_call(
        make_pick(groups, tiles, feat_dev, feat_dev // n_dp),
        out_shape=[
            jax.ShapeDtypeStruct((3 * tiles, LO), f32),
            jax.ShapeDtypeStruct((n_dp, groups * tiles + 1, 8, LO), f32),
        ],
        in_specs=[anywhere, anywhere, anywhere],
        out_specs=[vmem, vmem],
        scratch_shapes=[pltpu.SMEM((3,), i32), pltpu.VMEM((tiles, LO), bf16), pltpu.SemaphoreType.DMA((n_dp + 2,))],
        name="pick",
    )(split_feature, x, hess.reshape(tiles, LO))


def swap(value, axis, size, step):
    return lax.ppermute(value, axis, [(s, s ^ step) for s in range(size)])


def make_shards(n_dp, n_feat):
    def shards(fine_values, grad, hess, slab_rows, split_feature, split_bin):
        feat_dev, row_dev = fine_values.shape
        feats, tiles = feat_dev // n_dp, row_dev // LO
        groups = (feats + 7) // 8
        me = lax.axis_index("dp")
        both = ("dp", "feat")
        x = fine_values.reshape(n_dp, feats, tiles, LO)
        x = jnp.pad(x, ((0, 0), (0, groups * 8 - feats), (0, 0), (0, 0)))
        x = x.reshape(n_dp, groups, 8, tiles, LO).swapaxes(2, 3).reshape(n_dp, groups * tiles, 8, LO)
        share, x = pick_rows(x, hess, split_feature, groups, tiles, feat_dev)
        share = share + swap(share, "feat", n_feat, 1)
        g = grad.astype(f32).reshape(tiles, LO)
        share, g, block = lax.optimization_barrier((share, g, jnp.concatenate([share, g])))
        got = [swap(block, "dp", n_dp, 1)]
        for i in range(2, n_feat, 2):
            got.append(swap(share, "feat", n_feat, i))
            got.append(swap(share, both, n_dp * n_feat, n_feat + i))
        got = lax.optimization_barrier(got)
        mine, other, other_g = share, got[0][: 3 * tiles], got[0][3 * tiles :]
        for i in range(1, len(got), 2):
            mine, other = mine + got[i], other + got[i + 1]
        pair = jnp.stack([jnp.concatenate([mine, g]), jnp.concatenate([other, other_g])])
        pairs = [pair] + [swap(pair, "dp", n_dp, d) for d in range(2, n_dp, 2)]
        x = lax.all_to_all(x, "dp", 0, 0)
        bins = find_bins(x, slab_rows, groups, tiles)
        gains = route_and_sum(x, pairs, bins, slab_rows, split_bin, feats, groups, tiles)
        pieces = [gains] + [None] * (n_dp - 1)
        for d in [*range(n_dp - 2, 0, -2), 1]:
            pieces[d] = swap(gains, "dp", n_dp, d)
        for d in range(3, n_dp, 2):
            pieces[d] = swap(pieces[d - 1], "dp", n_dp, 1)
        whole = jnp.zeros((7, feat_dev, BINS), f32)
        order = [4, 2, 1] + [*range(6, n_dp, 2)] + [*range(3, n_dp, 2)]
        for d in [0] + [d for d in order if d < n_dp]:
            whole = lax.dynamic_update_slice_in_dim(whole, pieces[d], (me ^ d) * feats, 1)
        return whole

    return shards


def solution(mesh):
    return jax.shard_map(
        make_shards(mesh.shape["dp"], mesh.shape["feat"]),
        mesh=mesh,
        in_specs=(P("feat", "dp"), P("dp"), P("dp"), P(), P(), P()),
        out_specs=P(None, "feat", None),
        check_vma=False,
    )
```

```python
import jax
import jax.numpy as jnp
from jax import lax
from jax.experimental import pallas as pl
from jax.experimental.pallas import tpu as pltpu
from jax.sharding import PartitionSpec as P

FINE_BINS = 1024
BINS = 256
LO = 128
SIDE = 32
UPPER = 6
INNER = 48
GROUP = 16
f32 = jnp.float32
bf16 = jnp.bfloat16
i32 = jnp.int32


def dot_nt(a, b):
    return lax.dot_general(a, b, (((1,), (1,)), ((), ())), preferred_element_type=f32)


def dot_nn(a, b):
    return jnp.dot(a, b, preferred_element_type=f32)


def iota(shape, axis):
    return lax.broadcasted_iota(i32, shape, axis)


def to_bf16(x):
    return x.astype(f32).astype(bf16)


def bytes_of(x, axis):
    return jnp.concatenate([to_bf16((x >> (8 * i)) & 255) for i in range(4)], axis)


def coarse_of(whole):
    n = whole.shape[0]
    r, c = iota((LO, 2 * LO), 0), iota((LO, 2 * LO), 1)
    same = r // SIDE == (c % LO) // SIDE
    in_row = dot_nn(bytes_of(whole, 0), to_bf16(same & ((r < c) | (c >= LO)))).astype(i32)
    in_row = sum(in_row[i * n : (i + 1) * n] << (8 * i) for i in range(4))
    before, row_total = in_row[:, :LO], in_row[:, LO:]
    r, c = iota((2 * n, n), 0), iota((2 * n, n), 1)
    same = (r % n) // SIDE == c // SIDE
    over = dot_nn(to_bf16(same & ((c < r) | (r >= n))), bytes_of(row_total, 1)).astype(i32)
    over = sum(over[:, i * LO : (i + 1) * LO] << (8 * i) for i in range(4))
    total = over[n:]
    remainder = before + over[:n]
    quotient = jnp.zeros_like(remainder)
    for _ in range(BINS.bit_length() - 1):
        remainder = remainder * 2
        bit = remainder >= total
        remainder = jnp.where(bit, remainder - total, remainder)
        quotient = quotient * 2 + bit.astype(i32)
    return jnp.minimum(BINS - 1, quotient)


def fine_of(v):
    return jnp.clip(jnp.floor(v * FINE_BINS), 0, FINE_BINS - 1)


def split_by(t, side):
    upper = jnp.floor(t * (1.0 / side))
    return upper, t - upper * side


def spread(rows, f):
    return jnp.broadcast_to(rows[f : f + 1], (16, rows.shape[1])).astype(bf16)


def hot(row, count, value, zero):
    at = iota(row.shape, 0)
    return [jnp.where(row == to_bf16(at + 16 * j), value, zero) for j in range(count // 16)]


def list_blocks(slab_rows, list_ref, n_dp, tiles):
    used = 0
    for s in range(n_dp):
        for i in range(tiles):
            list_ref[used + i] = s * tiles + i
        used = used + (slab_rows[s] + LO - 1) // LO
    for i in range(GROUP - 1):
        list_ref[used + i] = n_dp * tiles
    return used


def list_shape(n_dp, tiles):
    return pltpu.SMEM((n_dp * tiles + GROUP,), i32)


def params():
    return pltpu.CompilerParams(vmem_limit_bytes=40 * 2**20)


def cost(flops):
    return pl.CostEstimate(flops=flops, bytes_accessed=2**20, transcendentals=0)


def make_bins(n_dp, groups, tiles):
    blocks = n_dp * tiles
    feats = groups * 8
    quads = feats // 4
    width = GROUP * LO

    def kernel(slab_rows, _, x_ref, *refs):
        hs, (o_ref, h_out, list_ref, h_ref, cnt_ref, cut_ref, map_ref) = refs[: n_dp // 2], refs[n_dp // 2 :]
        me = lax.axis_index("dp")
        used = list_blocks(slab_rows, list_ref, n_dp, tiles)
        row = iota((tiles, LO), 0) * LO + iota((tiles, LO), 1)
        for j in range(n_dp):
            s = me ^ j
            h = jnp.where(row < slab_rows[s], hs[j // 2][j % 2], 0.0)
            h_out[s] = h
            for i in range(tiles):
                h_ref[s * tiles + i] = jnp.broadcast_to(h[i : i + 1], (8, LO))
        h_ref[blocks] = jnp.zeros((8, LO), f32)
        cnt_ref[...] = jnp.zeros_like(cnt_ref)
        one, zero = jnp.ones((16, width), bf16), jnp.zeros((16, width), bf16)

        def fine_block(at):
            s, i = jnp.minimum(at // tiles, n_dp - 1), at % tiles
            return fine_of(jnp.concatenate([x_ref[s, g * tiles + i] for g in range(groups)], 0))

        def count(q, _):
            ts, hs = [], []
            for i in range(GROUP):
                at = list_ref[q * GROUP + i]
                ts.append(fine_block(at))
                hs.append(h_ref[at])
            h = jnp.concatenate(hs, 1)
            h = jnp.concatenate([h, h], 0).astype(bf16)
            upper, lower = split_by(jnp.concatenate(ts, 1), SIDE)
            for quad in range(quads):
                left, right = [], []
                for f in range(quad * 4, quad * 4 + 4):
                    left += hot(spread(upper, f), SIDE, h, zero)
                    right += hot(spread(lower, f), SIDE, one, zero)
                cnt_ref[quad] += dot_nt(jnp.concatenate(left, 0), jnp.concatenate(right, 0))
            return 0

        rounds = (used + GROUP - 1) // GROUP
        lax.fori_loop(0, rounds, count, 0)
        counts = []
        for quad in range(quads):
            lane = iota((SIDE, LO), 1) // SIDE
            mine = cnt_ref[quad, :SIDE]
            for i in range(1, 4):
                mine = jnp.where(lane == i, cnt_ref[quad, i * SIDE : (i + 1) * SIDE], mine)
            counts.append(mine)
        counts = jnp.concatenate(counts, 0)
        cut_ref[...] = coarse_of((counts * 16384.0).astype(i32)).astype(f32)
        lane = iota((quads * 8, LO), 1) // SIDE
        sub = iota((8, LO), 0)
        rows = [cut_ref[pl.ds(i, quads * 8, 4), :] for i in range(4)]
        words = [jnp.zeros((8, LO), i32) for _ in range(quads)]
        for q in range(4):
            table = jnp.zeros((quads * 8, LO), f32)
            for i in range(4):
                shift = (i - q) * SIDE % LO
                moved = pltpu.roll(rows[i], shift, 1) if shift else rows[i]
                table = jnp.where(lane == i, moved, table)
            for quad in range(quads):
                word = table[quad * 8 : quad * 8 + 8].astype(i32) << (sub % 4 * 8)
                word = word + pltpu.roll(word, 7, 0)
                word = word + pltpu.roll(word, 6, 0)
                word = pltpu.roll(word, q, 0) if q else word
                words[quad] = jnp.where(sub % 4 == q, word, words[quad])
        for quad in range(quads):
            map_ref[quad] = words[quad]
        upper_half = sub >= 4

        def look_up(q, _):
            for i in range(GROUP):
                at = list_ref[q * GROUP + i]
                fine = fine_block(at).astype(i32)
                for g in range(groups):
                    here = fine[g * 8 : g * 8 + 8]
                    turned = pltpu.roll(here, 4, 0)
                    found = []
                    for half in range(2):
                        t = jnp.where(upper_half, turned, here) if half == 0 else jnp.where(upper_half, here, turned)
                        word = jnp.take_along_axis(map_ref[g * 2 + half], t & (LO - 1), axis=1, mode="promise_in_bounds")
                        value = (word >> ((t >> 4) & 24)) & 255
                        value = jnp.where((t >= FINE_BINS // 2) == upper_half, value, 0)
                        found.append(value + pltpu.roll(value, 4, 0))
                    o_ref[at, g * 8 : g * 8 + 8, :] = jnp.where(upper_half, found[1], found[0]).astype(f32)
            return 0

        lax.fori_loop(0, rounds, look_up, 0)

    return kernel


def find_bins(x, hs, slab_rows, split_bin, groups, tiles):
    n_dp = x.shape[0]
    feats = groups * 8
    smem = pl.BlockSpec(memory_space=pltpu.SMEM)
    vmem = pl.BlockSpec(memory_space=pltpu.VMEM)
    return pl.pallas_call(
        make_bins(n_dp, groups, tiles),
        out_shape=[
            jax.ShapeDtypeStruct((n_dp * tiles + 1, feats, LO), f32),
            jax.ShapeDtypeStruct((n_dp, tiles, LO), f32),
        ],
        in_specs=[smem, smem] + [vmem] * (1 + len(hs)),
        out_specs=[vmem, vmem],
        scratch_shapes=[
            list_shape(n_dp, tiles),
            pltpu.VMEM((n_dp * tiles + 1, 8, LO), f32),
            pltpu.VMEM((feats // 4, LO, LO), f32),
            pltpu.VMEM((feats // 4 * SIDE, LO), f32),
            pltpu.VMEM((feats // 4, 8, LO), i32),
        ],
        compiler_params=params(),
        cost_estimate=cost(2 * 128 * 128 * n_dp * tiles * LO * feats // 4),
        name="bins",
    )(slab_rows, split_bin, x, *hs)


def make_route(n_dp, groups, tiles):
    blocks = n_dp * tiles

    def kernel(slab_rows, split_bin, x_ref, *refs):
        pairs, ch_ref, t_ref = refs[: n_dp // 2], refs[n_dp // 2], refs[n_dp // 2 + 1]
        me = lax.axis_index("dp")
        one, zero = jnp.ones((16, LO), bf16), jnp.zeros((16, LO), bf16)
        counts = jnp.zeros((LO, LO), f32)
        nothing = [zero] * (SIDE // 16)
        for j in range(n_dp):
            s = me ^ j
            row = iota((tiles, LO), 0) * LO + iota((tiles, LO), 1)
            live = row < slab_rows[s]
            t_ref[j, 3] = jnp.where(live, pairs[j // 2][j % 2, 3 * tiles :], 0.0)
            h = jnp.where(live, x_ref[s], 0.0)
            t_ref[j, 4] = h
            lefts, rights = [], []
            hs = [spread(h, i) for i in range(tiles)]
            for n in range(3):
                t = fine_of(pairs[j // 2][j % 2, n * tiles : (n + 1) * tiles])
                t_ref[j, n] = t
                upper, lower = split_by(t, SIDE)
                left = [jnp.concatenate(hot(spread(upper, i), SIDE, hs[i], zero), 0) for i in range(tiles)]
                right = [jnp.concatenate(hot(spread(lower, i), SIDE, one, zero), 0) for i in range(tiles)]
                lefts.append(jnp.concatenate(left, 1))
                rights.append(jnp.concatenate(right, 1))
            empty = jnp.zeros((SIDE, tiles * LO), bf16)
            counts += dot_nt(jnp.concatenate(lefts + [empty], 0), jnp.concatenate(rights + [empty], 0))
        lane = iota((SIDE, LO), 1)
        mine = counts[:SIDE]
        for n in range(1, 3):
            mine = jnp.where(lane // SIDE == n, counts[n * SIDE : (n + 1) * SIDE], mine)
        mine = jnp.where(lane < 3 * SIDE, (mine * 16384.0).astype(i32), 1)
        cut = coarse_of(mine)
        bound = jnp.where(lane < SIDE, split_bin[0], jnp.where(lane < 2 * SIDE, split_bin[1], split_bin[2]))
        below = jnp.sum(jnp.where(cut <= bound, 1.0, 0.0), axis=0, keepdims=True)
        lane = lane[:1]
        cuts = [jnp.sum(jnp.where(lane // SIDE == n, below, 0.0), axis=1, keepdims=True) for n in range(3)]
        ch_ref[blocks] = jnp.zeros((8, LO), f32)
        at = iota((8, LO), 0)
        for j in range(n_dp):
            s = me ^ j
            l0, l1, l2 = [t_ref[j, n] < cuts[n] for n in range(3)]
            leaf = jnp.where(l0, jnp.where(l1, 0, 1), jnp.where(l2, 2, 3))
            g, h = t_ref[j, 3], t_ref[j, 4]
            for i in range(tiles):
                gh = jnp.where(at < 4, jnp.broadcast_to(g[i : i + 1], (8, LO)), jnp.broadcast_to(h[i : i + 1], (8, LO)))
                here = at % 4 == jnp.broadcast_to(leaf[i : i + 1], (8, LO))
                ch_ref[s * tiles + i] = jnp.where(here, gh, 0.0)

    return kernel


def make_gains(n_dp, feats_all, feats, tiles):
    quads = feats_all // 4
    width = GROUP * LO
    lanes = 4 * UPPER * 8

    def kernel(slab_rows, bin_ref, ch_ref, o_ref, list_ref, acc_ref, cum_ref):
        used = list_blocks(slab_rows, list_ref, n_dp, tiles)
        acc_ref[...] = jnp.zeros_like(acc_ref)
        kk = [to_bf16(iota((16, width), 0) // 8 + 2 * j) for j in range(UPPER // 2)]
        one, zero = jnp.ones((16, width), bf16), jnp.zeros((16, width), bf16)
        lane = iota((INNER, lanes), 1) // (UPPER * 8)

        def add(q, _):
            bs, chs = [], []
            for i in range(GROUP):
                at = list_ref[q * GROUP + i]
                bs.append(bin_ref[at])
                chs.append(ch_ref[at])
            ch = jnp.concatenate(chs, 1)
            ch = jnp.concatenate([ch, ch], 0).astype(bf16)
            bins = jnp.concatenate(bs, 1)
            upper = jnp.floor((bins + 0.5) * (1.0 / INNER))
            lower = bins - upper * INNER
            for quad in range(quads):
                left, right = [], []
                for f in range(quad * 4, quad * 4 + 4):
                    left += hot(spread(lower, f), INNER, one, zero)
                    u = spread(upper, f)
                    right += [jnp.where(u == k, ch, zero) for k in kk]
                out = dot_nt(jnp.concatenate(left, 0), jnp.concatenate(right, 0))
                mine = out[:INNER]
                for i in range(1, 4):
                    mine = jnp.where(lane == i, out[i * INNER : (i + 1) * INNER], mine)
                acc_ref[quad, :INNER, :lanes] += mine
            return 0

        lax.fori_loop(0, (used + GROUP - 1) // GROUP, add, 0)
        r, c = iota((LO, 2 * LO), 0), iota((LO, 2 * LO), 1)
        upto = to_bf16(r <= c)
        at = iota((8, LO), 1)
        for quad in range(quads):
            acc = jnp.concatenate([jnp.transpose(acc_ref[quad, :, :LO]), jnp.transpose(acc_ref[quad, :, LO:])], 0)[:lanes]
            p0 = acc.astype(bf16)
            r1 = acc - p0.astype(f32)
            p1 = r1.astype(bf16)
            p2 = (r1 - p1.astype(f32)).astype(bf16)
            run = (dot_nn(p0, upto) + dot_nn(p1, upto)) + dot_nn(p2, upto)
            for i in range(4):
                f = quad * 4 + i
                if f >= feats:
                    break
                for t in range(BINS // LO):
                    gl = jnp.zeros((8, LO), f32)
                    for k in range(UPPER):
                        row = (i * UPPER + k) * 8
                        part, total = run[row : row + 8, :LO], run[row : row + 8, LO:]
                        s = INNER * k - LO * t
                        if s >= LO:
                            continue
                        if s <= -INNER:
                            part = total
                        elif s < 0:
                            part = jnp.where(at < LO + s, pltpu.roll(part, LO + s, 1), total)
                        elif s > 0:
                            part = jnp.where(at >= s, pltpu.roll(part, s, 1), 0.0)
                        gl = gl + part
                    for c in range(8):
                        cum_ref[c, f : f + 1, t * LO : t * LO + LO] = gl[c : c + 1]

        def score(g, h):
            return g * g / (h + 1.0)

        def nodes(at):
            leaves = [cum_ref[at + c] for c in range(4)]
            a, b = leaves[0] + leaves[1], leaves[2] + leaves[3]
            return [a + b, a, b] + leaves

        for i, (gl, hl) in enumerate(zip(nodes(0), nodes(4))):
            g, h = gl[:, BINS - 1 :], hl[:, BINS - 1 :]
            o_ref[i] = score(gl, hl) + score(g - gl, h - hl) - score(g, h)

    return kernel


def route_and_sum(x, pairs, bins, slab_rows, split_bin, feats, groups, tiles):
    n_dp = x.shape[0]
    blocks, feats_all = n_dp * tiles, groups * 8
    smem = pl.BlockSpec(memory_space=pltpu.SMEM)
    vmem = pl.BlockSpec(memory_space=pltpu.VMEM)
    route = make_route(n_dp, groups, tiles)
    sum_up = make_gains(n_dp, feats_all, feats, tiles)

    def kernel(slab_rows, split_bin, x_ref, bin_ref, *refs):
        o_ref, list_ref, ch_ref, t_ref, acc_ref, cum_ref = refs[n_dp // 2 :]
        route(slab_rows, split_bin, x_ref, *refs[: n_dp // 2], ch_ref, t_ref)
        sum_up(slab_rows, bin_ref, ch_ref, o_ref, list_ref, acc_ref, cum_ref)

    return pl.pallas_call(
        kernel,
        out_shape=jax.ShapeDtypeStruct((7, feats, BINS), f32),
        in_specs=[smem, smem] + [vmem] * (2 + len(pairs)),
        out_specs=vmem,
        scratch_shapes=[
            list_shape(n_dp, tiles),
            pltpu.VMEM((blocks + 1, 8, LO), f32),
            pltpu.VMEM((n_dp, 5, tiles, LO), f32),
            pltpu.VMEM((feats_all // 4, LO, 2 * LO), f32),
            pltpu.VMEM((8, feats, BINS), f32),
        ],
        compiler_params=params(),
        cost_estimate=cost(2 * 128 * 256 * blocks * LO * feats_all // 4),
        name="gains",
    )(slab_rows, split_bin, x, bins, *pairs)


def make_pick(groups, tiles, feat_dev, feats):
    def kernel(split_ref, x_ref, g_ref, h_ref, o_ref, g_out, h_out, split_feature, rows_ref, gh_ref, sems):
        me = lax.axis_index("feat")
        split_copy = pltpu.make_async_copy(split_ref, split_feature, sems.at[3])
        g_copy = pltpu.make_async_copy(g_ref, gh_ref.at[0], sems.at[4])
        h_copy = pltpu.make_async_copy(h_ref, gh_ref.at[1], sems.at[5])
        split_copy.start()
        g_copy.start()
        h_copy.start()
        split_copy.wait()
        at8 = iota((8, LO), 0)
        work = []
        for n in range(3):
            local = split_feature[n] - me * feat_dev
            owned = (local >= 0) & (local < feat_dev)
            at = jnp.clip(local, 0, feat_dev - 1)
            s, f = at // feats, at % feats
            copy = pltpu.make_async_copy(x_ref.at[s, pl.ds(f // 8 * tiles, tiles)], rows_ref.at[n], sems.at[n])
            copy.start()
            work.append((copy, (at8 == f % 8) & owned))
        g_copy.wait()
        h_copy.wait()
        g_out[...] = gh_ref[0].astype(f32)
        h_out[...] = gh_ref[1].astype(f32)
        for n, (copy, mine) in enumerate(work):
            copy.wait()
            for i in range(tiles):
                row = jnp.sum(jnp.where(mine, rows_ref[n, i], 0.0), axis=0, keepdims=True)
                o_ref[n * tiles + i : n * tiles + i + 1, :] = row

    return kernel


def pick_rows(x, grad, hess, split_feature, groups, tiles, feat_dev):
    n_dp = x.shape[0]
    anywhere = pl.BlockSpec(memory_space=pl.ANY)
    vmem = pl.BlockSpec(memory_space=pltpu.VMEM)
    return pl.pallas_call(
        make_pick(groups, tiles, feat_dev, feat_dev // n_dp),
        out_shape=[pltpu.VMEM((rows * tiles, LO), f32) for rows in (3, 1, 1)],
        in_specs=[anywhere] * 4,
        out_specs=[vmem] * 3,
        scratch_shapes=[
            pltpu.SMEM((3,), i32),
            pltpu.VMEM((3, tiles, 8, LO), f32),
            pltpu.VMEM((2, tiles, LO), bf16),
            pltpu.SemaphoreType.DMA((6,)),
        ],
        name="pick",
    )(split_feature, x, grad.reshape(tiles, LO), hess.reshape(tiles, LO))


def swap(value, axis, size, step):
    return lax.ppermute(value, axis, [(s, s ^ step) for s in range(size)])


def make_shards(n_dp, n_feat):
    def shards(fine_values, grad, hess, slab_rows, split_feature, split_bin):
        feat_dev, row_dev = fine_values.shape
        feats, tiles = feat_dev // n_dp, row_dev // LO
        groups = (feats + 7) // 8
        me = lax.axis_index("dp")
        both = ("dp", "feat")
        x = fine_values.reshape(n_dp, feats, tiles, LO)
        x = jnp.pad(x, ((0, 0), (0, groups * 8 - feats), (0, 0), (0, 0)))
        x = x.reshape(n_dp, groups, 8, tiles, LO).swapaxes(2, 3).reshape(n_dp, groups * tiles, 8, LO)
        share, g, h = pick_rows(x, grad, hess, split_feature, groups, tiles, feat_dev)
        share = share + swap(share, "feat", n_feat, 1)
        share, g, block = lax.optimization_barrier((share, g, jnp.concatenate([share, g])))
        got = [swap(block, "dp", n_dp, 1)]
        for i in range(2, n_feat, 2):
            got.append(swap(share, "feat", n_feat, i))
            got.append(swap(share, both, n_dp * n_feat, n_feat + i))
        got = lax.optimization_barrier(got)
        mine, other, other_g = share, got[0][: 3 * tiles], got[0][3 * tiles :]
        for i in range(1, len(got), 2):
            mine, other = mine + got[i], other + got[i + 1]
        pair = jnp.stack([jnp.concatenate([mine, g]), jnp.concatenate([other, other_g])])
        pairs = [pair] + [swap(pair, "dp", n_dp, d) for d in range(2, n_dp, 2)]
        x = lax.all_to_all(x, "dp", 0, 0)
        h = jnp.stack([h, swap(h, "dp", n_dp, 1)])
        hs = [h] + [swap(h, "dp", n_dp, d) for d in range(2, n_dp, 2)]
        bins, h = find_bins(x, hs, slab_rows, split_bin, groups, tiles)
        gains = route_and_sum(h, pairs, bins, slab_rows, split_bin, feats, groups, tiles)
        pieces = [gains] + [None] * (n_dp - 1)
        for d in [*range(n_dp - 2, 0, -2), 1]:
            pieces[d] = swap(gains, "dp", n_dp, d)
        for d in range(3, n_dp, 2):
            pieces[d] = swap(pieces[d - 1], "dp", n_dp, 1)
        whole = jnp.zeros((7, feat_dev, BINS), f32)
        order = [4, 2, 1] + [*range(6, n_dp, 2)] + [*range(3, n_dp, 2)]
        for d in [0] + [d for d in order if d < n_dp]:
            whole = lax.dynamic_update_slice_in_dim(whole, pieces[d], (me ^ d) * feats, 1)
        return whole

    return shards


def solution(mesh):
    return jax.shard_map(
        make_shards(mesh.shape["dp"], mesh.shape["feat"]),
        mesh=mesh,
        in_specs=(P("feat", "dp"), P("dp"), P("dp"), P(), P(), P()),
        out_specs=P(None, "feat", None),
        check_vma=False,
    )
```

```python
import jax
import jax.numpy as jnp
from jax import lax
from jax.experimental import pallas as pl
from jax.experimental.pallas import tpu as pltpu
from jax.sharding import PartitionSpec as P

FINE_BINS = 1024
BINS = 256
LO = 128
SIDE = 32
UPPER = 6
INNER = 48
GROUP = 16
f32 = jnp.float32
bf16 = jnp.bfloat16
i32 = jnp.int32


def dot_nt(a, b):
    return lax.dot_general(a, b, (((1,), (1,)), ((), ())), preferred_element_type=f32)


def dot_nn(a, b):
    return jnp.dot(a, b, preferred_element_type=f32)


def iota(shape, axis):
    return lax.broadcasted_iota(i32, shape, axis)


def to_bf16(x):
    return x.astype(f32).astype(bf16)


def bytes_of(x, axis):
    return jnp.concatenate([to_bf16((x >> (8 * i)) & 255) for i in range(4)], axis)


def coarse_of(whole):
    n = whole.shape[0]
    r, c = iota((LO, 2 * LO), 0), iota((LO, 2 * LO), 1)
    same = r // SIDE == (c % LO) // SIDE
    in_row = dot_nn(bytes_of(whole, 0), to_bf16(same & ((r < c) | (c >= LO)))).astype(i32)
    in_row = sum(in_row[i * n : (i + 1) * n] << (8 * i) for i in range(4))
    before, row_total = in_row[:, :LO], in_row[:, LO:]
    r, c = iota((2 * n, n), 0), iota((2 * n, n), 1)
    same = (r % n) // SIDE == c // SIDE
    over = dot_nn(to_bf16(same & ((c < r) | (r >= n))), bytes_of(row_total, 1)).astype(i32)
    over = sum(over[:, i * LO : (i + 1) * LO] << (8 * i) for i in range(4))
    total = over[n:]
    remainder = before + over[:n]
    quotient = jnp.zeros_like(remainder)
    for _ in range(BINS.bit_length() - 1):
        remainder = remainder * 2
        bit = remainder >= total
        remainder = jnp.where(bit, remainder - total, remainder)
        quotient = quotient * 2 + bit.astype(i32)
    return jnp.minimum(BINS - 1, quotient)


def fine_of(v):
    return jnp.clip(jnp.floor(v * FINE_BINS), 0, FINE_BINS - 1)


def split_by(t, side):
    upper = jnp.floor(t * (1.0 / side))
    return upper, t - upper * side


def spread(rows, f):
    return jnp.broadcast_to(rows[f : f + 1], (16, rows.shape[1])).astype(bf16)


def hot(row, count, value, zero):
    at = iota(row.shape, 0)
    return [jnp.where(row == to_bf16(at + 16 * j), value, zero) for j in range(count // 16)]


def list_blocks(slab_rows, list_ref, n_dp, tiles):
    used = 0
    for s in range(n_dp):
        for i in range(tiles):
            list_ref[used + i] = s * tiles + i
        used = used + (slab_rows[s] + LO - 1) // LO
    for i in range(GROUP - 1):
        list_ref[used + i] = n_dp * tiles
    return used


def over_blocks(used, body):
    whole = (used + GROUP // 2 - 1) // GROUP

    def long(q, _):
        body(q * GROUP, GROUP)
        return 0

    def short(q, _):
        body(whole * GROUP, GROUP // 2)
        return 0

    lax.fori_loop(0, whole, long, 0)
    lax.fori_loop(0, (used > whole * GROUP).astype(i32), short, 0)


def list_shape(n_dp, tiles):
    return pltpu.SMEM((n_dp * tiles + GROUP,), i32)


def params():
    return pltpu.CompilerParams(vmem_limit_bytes=40 * 2**20)


def cost(flops):
    return pl.CostEstimate(flops=flops, bytes_accessed=2**20, transcendentals=0)


def make_bins(n_dp, groups, tiles):
    blocks = n_dp * tiles
    feats = groups * 8
    quads = feats // 4

    def kernel(slab_rows, _, x_ref, *refs):
        hs, (o_ref, h_out, list_ref, h_ref, cnt_ref, cut_ref, map_ref) = refs[: n_dp // 2], refs[n_dp // 2 :]
        me = lax.axis_index("dp")
        used = list_blocks(slab_rows, list_ref, n_dp, tiles)
        row = iota((tiles, LO), 0) * LO + iota((tiles, LO), 1)
        for j in range(n_dp):
            s = me ^ j
            h = jnp.where(row < slab_rows[s], hs[j // 2][j % 2], 0.0)
            h_out[s] = h
            for i in range(tiles):
                h_ref[s * tiles + i] = jnp.broadcast_to(h[i : i + 1], (8, LO))
        h_ref[blocks] = jnp.zeros((8, LO), f32)
        cnt_ref[...] = jnp.zeros_like(cnt_ref)

        def fine_block(at):
            s, i = jnp.minimum(at // tiles, n_dp - 1), at % tiles
            return fine_of(jnp.concatenate([x_ref[s, g * tiles + i] for g in range(groups)], 0))

        def count(start, length):
            one, zero = jnp.ones((16, length * LO), bf16), jnp.zeros((16, length * LO), bf16)
            ts, hs = [], []
            for i in range(length):
                at = list_ref[start + i]
                ts.append(fine_block(at))
                hs.append(h_ref[at])
            h = jnp.concatenate(hs, 1)
            h = jnp.concatenate([h, h], 0).astype(bf16)
            upper, lower = split_by(jnp.concatenate(ts, 1), SIDE)
            for quad in range(quads):
                left, right = [], []
                for f in range(quad * 4, quad * 4 + 4):
                    left += hot(spread(upper, f), SIDE, h, zero)
                    right += hot(spread(lower, f), SIDE, one, zero)
                cnt_ref[quad] += dot_nt(jnp.concatenate(left, 0), jnp.concatenate(right, 0))

        over_blocks(used, count)
        counts = []
        for quad in range(quads):
            lane = iota((SIDE, LO), 1) // SIDE
            mine = cnt_ref[quad, :SIDE]
            for i in range(1, 4):
                mine = jnp.where(lane == i, cnt_ref[quad, i * SIDE : (i + 1) * SIDE], mine)
            counts.append(mine)
        counts = jnp.concatenate(counts, 0)
        cut_ref[...] = coarse_of((counts * 16384.0).astype(i32)).astype(f32)
        lane = iota((quads * 8, LO), 1) // SIDE
        sub = iota((8, LO), 0)
        rows = [cut_ref[pl.ds(i, quads * 8, 4), :] for i in range(4)]
        words = [jnp.zeros((8, LO), i32) for _ in range(quads)]
        for q in range(4):
            table = jnp.zeros((quads * 8, LO), f32)
            for i in range(4):
                shift = (i - q) * SIDE % LO
                moved = pltpu.roll(rows[i], shift, 1) if shift else rows[i]
                table = jnp.where(lane == i, moved, table)
            for quad in range(quads):
                word = table[quad * 8 : quad * 8 + 8].astype(i32) << (sub % 4 * 8)
                word = word + pltpu.roll(word, 7, 0)
                word = word + pltpu.roll(word, 6, 0)
                word = pltpu.roll(word, q, 0) if q else word
                words[quad] = jnp.where(sub % 4 == q, word, words[quad])
        for quad in range(quads):
            map_ref[quad] = words[quad]
        upper_half = sub >= 4

        def look_up(start, length):
            for i in range(length):
                at = list_ref[start + i]
                fine = fine_block(at).astype(i32)
                for g in range(groups):
                    here = fine[g * 8 : g * 8 + 8]
                    turned = pltpu.roll(here, 4, 0)
                    found = []
                    for half in range(2):
                        t = jnp.where(upper_half, turned, here) if half == 0 else jnp.where(upper_half, here, turned)
                        word = jnp.take_along_axis(map_ref[g * 2 + half], t & (LO - 1), axis=1, mode="promise_in_bounds")
                        value = (word >> ((t >> 4) & 24)) & 255
                        value = jnp.where((t >= FINE_BINS // 2) == upper_half, value, 0)
                        found.append(value + pltpu.roll(value, 4, 0))
                    o_ref[at, g * 8 : g * 8 + 8, :] = jnp.where(upper_half, found[1], found[0]).astype(f32)

        over_blocks(used, look_up)

    return kernel


def find_bins(x, hs, slab_rows, split_bin, groups, tiles):
    n_dp = x.shape[0]
    feats = groups * 8
    smem = pl.BlockSpec(memory_space=pltpu.SMEM)
    vmem = pl.BlockSpec(memory_space=pltpu.VMEM)
    return pl.pallas_call(
        make_bins(n_dp, groups, tiles),
        out_shape=[
            jax.ShapeDtypeStruct((n_dp * tiles + 1, feats, LO), f32),
            jax.ShapeDtypeStruct((n_dp, tiles, LO), f32),
        ],
        in_specs=[smem, smem] + [vmem] * (1 + len(hs)),
        out_specs=[vmem, vmem],
        scratch_shapes=[
            list_shape(n_dp, tiles),
            pltpu.VMEM((n_dp * tiles + 1, 8, LO), f32),
            pltpu.VMEM((feats // 4, LO, LO), f32),
            pltpu.VMEM((feats // 4 * SIDE, LO), f32),
            pltpu.VMEM((feats // 4, 8, LO), i32),
        ],
        compiler_params=params(),
        cost_estimate=cost(2 * 128 * 128 * n_dp * tiles * LO * feats // 4),
        name="bins",
    )(slab_rows, split_bin, x, *hs)


def make_route(n_dp, groups, tiles):
    blocks = n_dp * tiles

    def kernel(slab_rows, split_bin, x_ref, *refs):
        pairs, ch_ref, t_ref = refs[: n_dp // 2], refs[n_dp // 2], refs[n_dp // 2 + 1]
        me = lax.axis_index("dp")
        one, zero = jnp.ones((16, LO), bf16), jnp.zeros((16, LO), bf16)
        counts = jnp.zeros((3 * SIDE, 3 * SIDE), f32)
        for j in range(n_dp):
            s = me ^ j
            row = iota((tiles, LO), 0) * LO + iota((tiles, LO), 1)
            live = row < slab_rows[s]
            t_ref[j, 3] = jnp.where(live, pairs[j // 2][j % 2, 3 * tiles :], 0.0)
            h = jnp.where(live, x_ref[s], 0.0)
            t_ref[j, 4] = h
            lefts, rights = [], []
            hs = [spread(h, i) for i in range(tiles)]
            for n in range(3):
                t = fine_of(pairs[j // 2][j % 2, n * tiles : (n + 1) * tiles])
                t_ref[j, n] = t
                upper, lower = split_by(t, SIDE)
                left = [jnp.concatenate(hot(spread(upper, i), SIDE, hs[i], zero), 0) for i in range(tiles)]
                right = [jnp.concatenate(hot(spread(lower, i), SIDE, one, zero), 0) for i in range(tiles)]
                lefts.append(jnp.concatenate(left, 1))
                rights.append(jnp.concatenate(right, 1))
            counts += dot_nt(jnp.concatenate(lefts, 0), jnp.concatenate(rights, 0))
        lane = iota((SIDE, LO), 1)
        counts = jnp.concatenate([counts, jnp.zeros((3 * SIDE, LO - 3 * SIDE), f32)], 1)
        mine = counts[:SIDE]
        for n in range(1, 3):
            mine = jnp.where(lane // SIDE == n, counts[n * SIDE : (n + 1) * SIDE], mine)
        mine = jnp.where(lane < 3 * SIDE, (mine * 16384.0).astype(i32), 1)
        cut = coarse_of(mine)
        bound = jnp.where(lane < SIDE, split_bin[0], jnp.where(lane < 2 * SIDE, split_bin[1], split_bin[2]))
        below = jnp.sum(jnp.where(cut <= bound, 1.0, 0.0), axis=0, keepdims=True)
        lane = lane[:1]
        cuts = [jnp.sum(jnp.where(lane // SIDE == n, below, 0.0), axis=1, keepdims=True) for n in range(3)]
        ch_ref[blocks] = jnp.zeros((8, LO), f32)
        at = iota((8, LO), 0)
        for j in range(n_dp):
            s = me ^ j
            l0, l1, l2 = [t_ref[j, n] < cuts[n] for n in range(3)]
            leaf = jnp.where(l0, jnp.where(l1, 0, 1), jnp.where(l2, 2, 3))
            g, h = t_ref[j, 3], t_ref[j, 4]
            for i in range(tiles):
                gh = jnp.where(at < 4, jnp.broadcast_to(g[i : i + 1], (8, LO)), jnp.broadcast_to(h[i : i + 1], (8, LO)))
                here = at % 4 == jnp.broadcast_to(leaf[i : i + 1], (8, LO))
                ch_ref[s * tiles + i] = jnp.where(here, gh, 0.0)

    return kernel


def make_gains(n_dp, feats_all, feats, tiles):
    quads = feats_all // 4
    lanes = 4 * UPPER * 8

    def kernel(slab_rows, bin_ref, ch_ref, o_ref, list_ref, acc_ref, cum_ref):
        used = list_blocks(slab_rows, list_ref, n_dp, tiles)
        acc_ref[...] = jnp.zeros_like(acc_ref)
        lane = iota((INNER, lanes), 1) // (UPPER * 8)

        def add(start, length):
            width = length * LO
            kk = [to_bf16(iota((16, width), 0) // 8 + 2 * j) for j in range(UPPER // 2)]
            one, zero = jnp.ones((16, width), bf16), jnp.zeros((16, width), bf16)
            bs, chs = [], []
            for i in range(length):
                at = list_ref[start + i]
                bs.append(bin_ref[at])
                chs.append(ch_ref[at])
            ch = jnp.concatenate(chs, 1)
            ch = jnp.concatenate([ch, ch], 0).astype(bf16)
            bins = jnp.concatenate(bs, 1)
            upper = jnp.floor((bins + 0.5) * (1.0 / INNER))
            lower = bins - upper * INNER
            for quad in range(quads):
                left, right = [], []
                for f in range(quad * 4, quad * 4 + 4):
                    left += hot(spread(lower, f), INNER, one, zero)
                    u = spread(upper, f)
                    right += [jnp.where(u == k, ch, zero) for k in kk]
                out = dot_nt(jnp.concatenate(left, 0), jnp.concatenate(right, 0))
                mine = out[:INNER]
                for i in range(1, 4):
                    mine = jnp.where(lane == i, out[i * INNER : (i + 1) * INNER], mine)
                acc_ref[quad, :INNER, :lanes] += mine

        over_blocks(used, add)
        r, c = iota((LO, 2 * LO), 0), iota((LO, 2 * LO), 1)
        upto = to_bf16(r <= c)
        at = iota((8, LO), 1)
        for quad in range(quads):
            acc = jnp.concatenate([jnp.transpose(acc_ref[quad, :, :LO]), jnp.transpose(acc_ref[quad, :, LO:])], 0)[:lanes]
            p0 = acc.astype(bf16)
            r1 = acc - p0.astype(f32)
            p1 = r1.astype(bf16)
            p2 = (r1 - p1.astype(f32)).astype(bf16)
            run = (dot_nn(p0, upto) + dot_nn(p1, upto)) + dot_nn(p2, upto)
            for i in range(4):
                f = quad * 4 + i
                if f >= feats:
                    break
                for t in range(BINS // LO):
                    gl = jnp.zeros((8, LO), f32)
                    for k in range(UPPER):
                        row = (i * UPPER + k) * 8
                        part, total = run[row : row + 8, :LO], run[row : row + 8, LO:]
                        s = INNER * k - LO * t
                        if s >= LO:
                            continue
                        if s <= -INNER:
                            part = total
                        elif s < 0:
                            part = jnp.where(at < LO + s, pltpu.roll(part, LO + s, 1), total)
                        elif s > 0:
                            part = jnp.where(at >= s, pltpu.roll(part, s, 1), 0.0)
                        gl = gl + part
                    for c in range(8):
                        cum_ref[c, f : f + 1, t * LO : t * LO + LO] = gl[c : c + 1]

        def score(g, h):
            return g * g / (h + 1.0)

        def nodes(at):
            leaves = [cum_ref[at + c] for c in range(4)]
            a, b = leaves[0] + leaves[1], leaves[2] + leaves[3]
            return [a + b, a, b] + leaves

        for i, (gl, hl) in enumerate(zip(nodes(0), nodes(4))):
            g, h = gl[:, BINS - 1 :], hl[:, BINS - 1 :]
            o_ref[i] = score(gl, hl) + score(g - gl, h - hl) - score(g, h)

    return kernel


def route_and_sum(x, pairs, bins, slab_rows, split_bin, feats, groups, tiles):
    n_dp = x.shape[0]
    blocks, feats_all = n_dp * tiles, groups * 8
    smem = pl.BlockSpec(memory_space=pltpu.SMEM)
    vmem = pl.BlockSpec(memory_space=pltpu.VMEM)
    route = make_route(n_dp, groups, tiles)
    sum_up = make_gains(n_dp, feats_all, feats, tiles)

    def kernel(slab_rows, split_bin, x_ref, bin_ref, *refs):
        o_ref, list_ref, ch_ref, t_ref, acc_ref, cum_ref = refs[n_dp // 2 :]
        route(slab_rows, split_bin, x_ref, *refs[: n_dp // 2], ch_ref, t_ref)
        sum_up(slab_rows, bin_ref, ch_ref, o_ref, list_ref, acc_ref, cum_ref)

    return pl.pallas_call(
        kernel,
        out_shape=jax.ShapeDtypeStruct((7, feats, BINS), f32),
        in_specs=[smem, smem] + [vmem] * (2 + len(pairs)),
        out_specs=vmem,
        scratch_shapes=[
            list_shape(n_dp, tiles),
            pltpu.VMEM((blocks + 1, 8, LO), f32),
            pltpu.VMEM((n_dp, 5, tiles, LO), f32),
            pltpu.VMEM((feats_all // 4, LO, 2 * LO), f32),
            pltpu.VMEM((8, feats, BINS), f32),
        ],
        compiler_params=params(),
        cost_estimate=cost(2 * 128 * 256 * blocks * LO * feats_all // 4),
        name="gains",
    )(slab_rows, split_bin, x, bins, *pairs)


def make_pick(groups, tiles, feat_dev, feats):
    def kernel(split_ref, x_ref, g_ref, h_ref, o_ref, g_out, h_out, split_feature, rows_ref, gh_ref, sems):
        me = lax.axis_index("feat")
        split_copy = pltpu.make_async_copy(split_ref, split_feature, sems.at[3])
        g_copy = pltpu.make_async_copy(g_ref, gh_ref.at[0], sems.at[4])
        h_copy = pltpu.make_async_copy(h_ref, gh_ref.at[1], sems.at[5])
        split_copy.start()
        g_copy.start()
        h_copy.start()
        split_copy.wait()
        at8 = iota((8, LO), 0)
        work = []
        for n in range(3):
            local = split_feature[n] - me * feat_dev
            owned = (local >= 0) & (local < feat_dev)
            at = jnp.clip(local, 0, feat_dev - 1)
            s, f = at // feats, at % feats
            copy = pltpu.make_async_copy(x_ref.at[s, pl.ds(f // 8 * tiles, tiles)], rows_ref.at[n], sems.at[n])
            copy.start()
            work.append((copy, (at8 == f % 8) & owned))
        g_copy.wait()
        h_copy.wait()
        g_out[...] = gh_ref[0].astype(f32)
        h_out[...] = gh_ref[1].astype(f32)
        for n, (copy, mine) in enumerate(work):
            copy.wait()
            for i in range(tiles):
                row = jnp.sum(jnp.where(mine, rows_ref[n, i], 0.0), axis=0, keepdims=True)
                o_ref[n * tiles + i : n * tiles + i + 1, :] = row

    return kernel


def pick_rows(x, grad, hess, split_feature, groups, tiles, feat_dev):
    n_dp = x.shape[0]
    anywhere = pl.BlockSpec(memory_space=pl.ANY)
    vmem = pl.BlockSpec(memory_space=pltpu.VMEM)
    return pl.pallas_call(
        make_pick(groups, tiles, feat_dev, feat_dev // n_dp),
        out_shape=[pltpu.VMEM((rows * tiles, LO), f32) for rows in (3, 1, 1)],
        in_specs=[anywhere] * 4,
        out_specs=[vmem] * 3,
        scratch_shapes=[
            pltpu.SMEM((3,), i32),
            pltpu.VMEM((3, tiles, 8, LO), f32),
            pltpu.VMEM((2, tiles, LO), bf16),
            pltpu.SemaphoreType.DMA((6,)),
        ],
        name="pick",
    )(split_feature, x, grad.reshape(tiles, LO), hess.reshape(tiles, LO))


def swap(value, axis, size, step):
    return lax.ppermute(value, axis, [(s, s ^ step) for s in range(size)])


def make_shards(n_dp, n_feat):
    def shards(fine_values, grad, hess, slab_rows, split_feature, split_bin):
        feat_dev, row_dev = fine_values.shape
        feats, tiles = feat_dev // n_dp, row_dev // LO
        groups = (feats + 7) // 8
        me = lax.axis_index("dp")
        both = ("dp", "feat")
        x = fine_values.reshape(n_dp, feats, tiles, LO)
        x = jnp.pad(x, ((0, 0), (0, groups * 8 - feats), (0, 0), (0, 0)))
        x = x.reshape(n_dp, groups, 8, tiles, LO).swapaxes(2, 3).reshape(n_dp, groups * tiles, 8, LO)
        share, g, h = pick_rows(x, grad, hess, split_feature, groups, tiles, feat_dev)
        share = share + swap(share, "feat", n_feat, 1)
        share, g, block = lax.optimization_barrier((share, g, jnp.concatenate([share, g])))
        got = [swap(block, "dp", n_dp, 1)]
        for i in range(2, n_feat, 2):
            got.append(swap(share, "feat", n_feat, i))
            got.append(swap(share, both, n_dp * n_feat, n_feat + i))
        got = lax.optimization_barrier(got)
        mine, other, other_g = share, got[0][: 3 * tiles], got[0][3 * tiles :]
        for i in range(1, len(got), 2):
            mine, other = mine + got[i], other + got[i + 1]
        pair = jnp.stack([jnp.concatenate([mine, g]), jnp.concatenate([other, other_g])])
        pairs = [pair] + [swap(pair, "dp", n_dp, d) for d in range(2, n_dp, 2)]
        x = lax.all_to_all(x, "dp", 0, 0)
        h = jnp.stack([h, swap(h, "dp", n_dp, 1)])
        hs = [h] + [swap(h, "dp", n_dp, d) for d in range(2, n_dp, 2)]
        bins, h = find_bins(x, hs, slab_rows, split_bin, groups, tiles)
        gains = route_and_sum(h, pairs, bins, slab_rows, split_bin, feats, groups, tiles)
        pieces = [gains] + [None] * (n_dp - 1)
        for d in [*range(n_dp - 2, 0, -2), 1]:
            pieces[d] = swap(gains, "dp", n_dp, d)
        for d in range(3, n_dp, 2):
            pieces[d] = swap(pieces[d - 1], "dp", n_dp, 1)
        whole = jnp.zeros((7, feat_dev, BINS), f32)
        order = [4, 2] + [*range(6, n_dp, 2)] + [1] + [*range(3, n_dp, 2)]
        for d in [0] + [d for d in order if d < n_dp]:
            whole = lax.dynamic_update_slice_in_dim(whole, pieces[d], (me ^ d) * feats, 1)
        return whole

    return shards


def solution(mesh):
    return jax.shard_map(
        make_shards(mesh.shape["dp"], mesh.shape["feat"]),
        mesh=mesh,
        in_specs=(P("feat", "dp"), P("dp"), P("dp"), P(), P(), P()),
        out_specs=P(None, "feat", None),
        check_vma=False,
    )
```

```python
import jax
import jax.numpy as jnp
from jax import lax
from jax.experimental import pallas as pl
from jax.experimental.pallas import tpu as pltpu
from jax.sharding import PartitionSpec as P

FINE_BINS = 1024
BINS = 256
LO = 128
SIDE = 32
UPPER = 6
INNER = 48
GROUP = 32
f32 = jnp.float32
bf16 = jnp.bfloat16
i32 = jnp.int32


def dot_nt(a, b):
    return lax.dot_general(a, b, (((1,), (1,)), ((), ())), preferred_element_type=f32)


def dot_nn(a, b):
    return jnp.dot(a, b, preferred_element_type=f32)


def iota(shape, axis):
    return lax.broadcasted_iota(i32, shape, axis)


def to_bf16(x):
    return x.astype(f32).astype(bf16)


def bytes_of(x, axis):
    return jnp.concatenate([to_bf16((x >> (8 * i)) & 255) for i in range(4)], axis)


def coarse_of(whole):
    n = whole.shape[0]
    r, c = iota((LO, 2 * LO), 0), iota((LO, 2 * LO), 1)
    same = r // SIDE == (c % LO) // SIDE
    in_row = dot_nn(bytes_of(whole, 0), to_bf16(same & ((r < c) | (c >= LO)))).astype(i32)
    in_row = sum(in_row[i * n : (i + 1) * n] << (8 * i) for i in range(4))
    before, row_total = in_row[:, :LO], in_row[:, LO:]
    r, c = iota((2 * n, n), 0), iota((2 * n, n), 1)
    same = (r % n) // SIDE == c // SIDE
    over = dot_nn(to_bf16(same & ((c < r) | (r >= n))), bytes_of(row_total, 1)).astype(i32)
    over = sum(over[:, i * LO : (i + 1) * LO] << (8 * i) for i in range(4))
    total = over[n:]
    remainder = before + over[:n]
    quotient = jnp.zeros_like(remainder)
    for _ in range(BINS.bit_length() - 1):
        remainder = remainder * 2
        bit = remainder >= total
        remainder = jnp.where(bit, remainder - total, remainder)
        quotient = quotient * 2 + bit.astype(i32)
    return jnp.minimum(BINS - 1, quotient)


def fine_of(v):
    return jnp.clip(jnp.floor(v * FINE_BINS), 0, FINE_BINS - 1)


def split_by(t, side):
    upper = jnp.floor(t * (1.0 / side))
    return upper, t - upper * side


def spread(rows, f):
    return jnp.broadcast_to(rows[f : f + 1], (16, rows.shape[1])).astype(bf16)


def hot(row, count, value, zero):
    at = iota(row.shape, 0)
    return [jnp.where(row == to_bf16(at + 16 * j), value, zero) for j in range(count // 16)]


def list_blocks(slab_rows, list_ref, n_dp, tiles):
    used = 0
    for s in range(n_dp):
        for i in range(tiles):
            list_ref[used + i] = s * tiles + i
        used = used + (slab_rows[s] + LO - 1) // LO
    for i in range(GROUP - 1):
        list_ref[used + i] = n_dp * tiles
    return used


def over_blocks(used, body):
    unit = GROUP // 4
    units = (used + unit - 1) // unit

    def run(start, count):
        def step(q, _):
            body((start + q * count) * unit, count * unit)
            return 0

        return step

    lax.fori_loop(0, units // 4, run(0, 4), 0)
    lax.fori_loop(0, units // 2 % 2, run(units // 4 * 4, 2), 0)
    lax.fori_loop(0, units % 2, run(units // 2 * 2, 1), 0)


def list_shape(n_dp, tiles):
    return pltpu.SMEM((n_dp * tiles + GROUP,), i32)


def params():
    return pltpu.CompilerParams(vmem_limit_bytes=40 * 2**20)


def cost(flops):
    return pl.CostEstimate(flops=flops, bytes_accessed=2**20, transcendentals=0)


def make_bins(n_dp, groups, tiles):
    blocks = n_dp * tiles
    feats = groups * 8
    quads = feats // 4

    def kernel(slab_rows, _, x_ref, *refs):
        hs, (o_ref, h_out, list_ref, h_ref, cnt_ref, cut_ref, map_ref) = refs[: n_dp // 2], refs[n_dp // 2 :]
        me = lax.axis_index("dp")
        used = list_blocks(slab_rows, list_ref, n_dp, tiles)
        row = iota((tiles, LO), 0) * LO + iota((tiles, LO), 1)
        for j in range(n_dp):
            s = me ^ j
            h = jnp.where(row < slab_rows[s], hs[j // 2][j % 2], 0.0)
            h_out[s] = h
            for i in range(tiles):
                h_ref[s * tiles + i] = jnp.broadcast_to(h[i : i + 1], (8, LO))
        h_ref[blocks] = jnp.zeros((8, LO), f32)
        cnt_ref[...] = jnp.zeros_like(cnt_ref)

        def fine_block(at):
            s, i = jnp.minimum(at // tiles, n_dp - 1), at % tiles
            return fine_of(jnp.concatenate([x_ref[s, g * tiles + i] for g in range(groups)], 0))

        def count(start, length):
            one, zero = jnp.ones((16, length * LO), bf16), jnp.zeros((16, length * LO), bf16)
            ts, hs = [], []
            for i in range(length):
                at = list_ref[start + i]
                ts.append(fine_block(at))
                hs.append(h_ref[at])
            h = jnp.concatenate(hs, 1)
            h = jnp.concatenate([h, h], 0).astype(bf16)
            upper, lower = split_by(jnp.concatenate(ts, 1), SIDE)
            for quad in range(quads):
                left, right = [], []
                for f in range(quad * 4, quad * 4 + 4):
                    left += hot(spread(upper, f), SIDE, h, zero)
                    right += hot(spread(lower, f), SIDE, one, zero)
                cnt_ref[quad] += dot_nt(jnp.concatenate(left, 0), jnp.concatenate(right, 0))

        over_blocks(used, count)
        counts = []
        for quad in range(quads):
            lane = iota((SIDE, LO), 1) // SIDE
            mine = cnt_ref[quad, :SIDE]
            for i in range(1, 4):
                mine = jnp.where(lane == i, cnt_ref[quad, i * SIDE : (i + 1) * SIDE], mine)
            counts.append(mine)
        counts = jnp.concatenate(counts, 0)
        cut_ref[...] = coarse_of((counts * 16384.0).astype(i32)).astype(f32)
        lane = iota((quads * 8, LO), 1) // SIDE
        sub = iota((8, LO), 0)
        rows = [cut_ref[pl.ds(i, quads * 8, 4), :] for i in range(4)]
        words = [jnp.zeros((8, LO), i32) for _ in range(quads)]
        for q in range(4):
            table = jnp.zeros((quads * 8, LO), f32)
            for i in range(4):
                shift = (i - q) * SIDE % LO
                moved = pltpu.roll(rows[i], shift, 1) if shift else rows[i]
                table = jnp.where(lane == i, moved, table)
            for quad in range(quads):
                word = table[quad * 8 : quad * 8 + 8].astype(i32) << (sub % 4 * 8)
                word = word + pltpu.roll(word, 7, 0)
                word = word + pltpu.roll(word, 6, 0)
                word = pltpu.roll(word, q, 0) if q else word
                words[quad] = jnp.where(sub % 4 == q, word, words[quad])
        for quad in range(quads):
            map_ref[quad] = words[quad]
        upper_half = sub >= 4

        def look_up(start, length):
            for i in range(length):
                at = list_ref[start + i]
                fine = fine_block(at).astype(i32)
                for g in range(groups):
                    here = fine[g * 8 : g * 8 + 8]
                    turned = pltpu.roll(here, 4, 0)
                    found = []
                    for half in range(2):
                        t = jnp.where(upper_half, turned, here) if half == 0 else jnp.where(upper_half, here, turned)
                        word = jnp.take_along_axis(map_ref[g * 2 + half], t & (LO - 1), axis=1, mode="promise_in_bounds")
                        value = (word >> ((t >> 4) & 24)) & 255
                        value = jnp.where((t >= FINE_BINS // 2) == upper_half, value, 0)
                        found.append(value + pltpu.roll(value, 4, 0))
                    o_ref[at, g * 8 : g * 8 + 8, :] = jnp.where(upper_half, found[1], found[0]).astype(f32)

        over_blocks(used, look_up)

    return kernel


def find_bins(x, hs, slab_rows, split_bin, groups, tiles):
    n_dp = x.shape[0]
    feats = groups * 8
    smem = pl.BlockSpec(memory_space=pltpu.SMEM)
    vmem = pl.BlockSpec(memory_space=pltpu.VMEM)
    return pl.pallas_call(
        make_bins(n_dp, groups, tiles),
        out_shape=[
            jax.ShapeDtypeStruct((n_dp * tiles + 1, feats, LO), f32),
            jax.ShapeDtypeStruct((n_dp, tiles, LO), f32),
        ],
        in_specs=[smem, smem] + [vmem] * (1 + len(hs)),
        out_specs=[vmem, vmem],
        scratch_shapes=[
            list_shape(n_dp, tiles),
            pltpu.VMEM((n_dp * tiles + 1, 8, LO), f32),
            pltpu.VMEM((feats // 4, LO, LO), f32),
            pltpu.VMEM((feats // 4 * SIDE, LO), f32),
            pltpu.VMEM((feats // 4, 8, LO), i32),
        ],
        compiler_params=params(),
        cost_estimate=cost(2 * 128 * 128 * n_dp * tiles * LO * feats // 4),
        name="bins",
    )(slab_rows, split_bin, x, *hs)


def make_route(n_dp, groups, tiles):
    blocks = n_dp * tiles

    def kernel(slab_rows, split_bin, x_ref, *refs):
        pairs, ch_ref, t_ref = refs[: n_dp // 2], refs[n_dp // 2], refs[n_dp // 2 + 1]
        me = lax.axis_index("dp")
        one, zero = jnp.ones((16, LO), bf16), jnp.zeros((16, LO), bf16)
        counts = jnp.zeros((3 * SIDE, 3 * SIDE), f32)
        for j in range(n_dp):
            s = me ^ j
            row = iota((tiles, LO), 0) * LO + iota((tiles, LO), 1)
            live = row < slab_rows[s]
            t_ref[j, 3] = jnp.where(live, pairs[j // 2][j % 2, 3 * tiles :], 0.0)
            h = jnp.where(live, x_ref[s], 0.0)
            t_ref[j, 4] = h
            lefts, rights = [], []
            hs = [spread(h, i) for i in range(tiles)]
            for n in range(3):
                t = fine_of(pairs[j // 2][j % 2, n * tiles : (n + 1) * tiles])
                t_ref[j, n] = t
                upper, lower = split_by(t, SIDE)
                left = [jnp.concatenate(hot(spread(upper, i), SIDE, hs[i], zero), 0) for i in range(tiles)]
                right = [jnp.concatenate(hot(spread(lower, i), SIDE, one, zero), 0) for i in range(tiles)]
                lefts.append(jnp.concatenate(left, 1))
                rights.append(jnp.concatenate(right, 1))
            counts += dot_nt(jnp.concatenate(lefts, 0), jnp.concatenate(rights, 0))
        lane = iota((SIDE, LO), 1)
        counts = jnp.concatenate([counts, jnp.zeros((3 * SIDE, LO - 3 * SIDE), f32)], 1)
        mine = counts[:SIDE]
        for n in range(1, 3):
            mine = jnp.where(lane // SIDE == n, counts[n * SIDE : (n + 1) * SIDE], mine)
        mine = jnp.where(lane < 3 * SIDE, (mine * 16384.0).astype(i32), 1)
        cut = coarse_of(mine)
        bound = jnp.where(lane < SIDE, split_bin[0], jnp.where(lane < 2 * SIDE, split_bin[1], split_bin[2]))
        below = jnp.sum(jnp.where(cut <= bound, 1.0, 0.0), axis=0, keepdims=True)
        lane = lane[:1]
        cuts = [jnp.sum(jnp.where(lane // SIDE == n, below, 0.0), axis=1, keepdims=True) for n in range(3)]
        ch_ref[blocks] = jnp.zeros((8, LO), f32)
        at = iota((8, LO), 0)
        for j in range(n_dp):
            s = me ^ j
            l0, l1, l2 = [t_ref[j, n] < cuts[n] for n in range(3)]
            leaf = jnp.where(l0, jnp.where(l1, 0, 1), jnp.where(l2, 2, 3))
            g, h = t_ref[j, 3], t_ref[j, 4]
            for i in range(tiles):
                gh = jnp.where(at < 4, jnp.broadcast_to(g[i : i + 1], (8, LO)), jnp.broadcast_to(h[i : i + 1], (8, LO)))
                here = at % 4 == jnp.broadcast_to(leaf[i : i + 1], (8, LO))
                ch_ref[s * tiles + i] = jnp.where(here, gh, 0.0)

    return kernel


def make_gains(n_dp, feats_all, feats, tiles):
    quads = feats_all // 4
    lanes = 4 * UPPER * 8

    def kernel(slab_rows, bin_ref, ch_ref, o_ref, list_ref, acc_ref, cum_ref):
        used = list_blocks(slab_rows, list_ref, n_dp, tiles)
        acc_ref[...] = jnp.zeros_like(acc_ref)
        lane = iota((INNER, lanes), 1) // (UPPER * 8)

        def add(start, length):
            width = length * LO
            kk = [to_bf16(iota((16, width), 0) // 8 + 2 * j) for j in range(UPPER // 2)]
            one, zero = jnp.ones((16, width), bf16), jnp.zeros((16, width), bf16)
            bs, chs = [], []
            for i in range(length):
                at = list_ref[start + i]
                bs.append(bin_ref[at])
                chs.append(ch_ref[at])
            ch = jnp.concatenate(chs, 1)
            ch = jnp.concatenate([ch, ch], 0).astype(bf16)
            bins = jnp.concatenate(bs, 1)
            upper = jnp.floor((bins + 0.5) * (1.0 / INNER))
            lower = bins - upper * INNER
            for quad in range(quads):
                left, right = [], []
                for f in range(quad * 4, quad * 4 + 4):
                    left += hot(spread(lower, f), INNER, one, zero)
                    u = spread(upper, f)
                    right += [jnp.where(u == k, ch, zero) for k in kk]
                out = dot_nt(jnp.concatenate(left, 0), jnp.concatenate(right, 0))
                mine = out[:INNER]
                for i in range(1, 4):
                    mine = jnp.where(lane == i, out[i * INNER : (i + 1) * INNER], mine)
                acc_ref[quad, :INNER, :lanes] += mine

        over_blocks(used, add)
        r, c = iota((LO, 2 * LO), 0), iota((LO, 2 * LO), 1)
        upto = to_bf16(r <= c)
        at = iota((8, LO), 1)
        for quad in range(quads):
            acc = jnp.concatenate([jnp.transpose(acc_ref[quad, :, :LO]), jnp.transpose(acc_ref[quad, :, LO:])], 0)[:lanes]
            p0 = acc.astype(bf16)
            r1 = acc - p0.astype(f32)
            p1 = r1.astype(bf16)
            p2 = (r1 - p1.astype(f32)).astype(bf16)
            run = (dot_nn(p0, upto) + dot_nn(p1, upto)) + dot_nn(p2, upto)
            for i in range(4):
                f = quad * 4 + i
                if f >= feats:
                    break
                for t in range(BINS // LO):
                    gl = jnp.zeros((8, LO), f32)
                    for k in range(UPPER):
                        row = (i * UPPER + k) * 8
                        part, total = run[row : row + 8, :LO], run[row : row + 8, LO:]
                        s = INNER * k - LO * t
                        if s >= LO:
                            continue
                        if s <= -INNER:
                            part = total
                        elif s < 0:
                            part = jnp.where(at < LO + s, pltpu.roll(part, LO + s, 1), total)
                        elif s > 0:
                            part = jnp.where(at >= s, pltpu.roll(part, s, 1), 0.0)
                        gl = gl + part
                    for c in range(8):
                        cum_ref[c, f : f + 1, t * LO : t * LO + LO] = gl[c : c + 1]

        def score(g, h):
            return g * g / (h + 1.0)

        def nodes(at):
            leaves = [cum_ref[at + c] for c in range(4)]
            a, b = leaves[0] + leaves[1], leaves[2] + leaves[3]
            return [a + b, a, b] + leaves

        for i, (gl, hl) in enumerate(zip(nodes(0), nodes(4))):
            g, h = gl[:, BINS - 1 :], hl[:, BINS - 1 :]
            o_ref[i] = score(gl, hl) + score(g - gl, h - hl) - score(g, h)

    return kernel


def route_and_sum(x, pairs, bins, slab_rows, split_bin, feats, groups, tiles):
    n_dp = x.shape[0]
    blocks, feats_all = n_dp * tiles, groups * 8
    smem = pl.BlockSpec(memory_space=pltpu.SMEM)
    vmem = pl.BlockSpec(memory_space=pltpu.VMEM)
    route = make_route(n_dp, groups, tiles)
    sum_up = make_gains(n_dp, feats_all, feats, tiles)

    def kernel(slab_rows, split_bin, x_ref, bin_ref, *refs):
        o_ref, list_ref, ch_ref, t_ref, acc_ref, cum_ref = refs[n_dp // 2 :]
        route(slab_rows, split_bin, x_ref, *refs[: n_dp // 2], ch_ref, t_ref)
        sum_up(slab_rows, bin_ref, ch_ref, o_ref, list_ref, acc_ref, cum_ref)

    return pl.pallas_call(
        kernel,
        out_shape=jax.ShapeDtypeStruct((7, feats, BINS), f32),
        in_specs=[smem, smem] + [vmem] * (2 + len(pairs)),
        out_specs=vmem,
        scratch_shapes=[
            list_shape(n_dp, tiles),
            pltpu.VMEM((blocks + 1, 8, LO), f32),
            pltpu.VMEM((n_dp, 5, tiles, LO), f32),
            pltpu.VMEM((feats_all // 4, LO, 2 * LO), f32),
            pltpu.VMEM((8, feats, BINS), f32),
        ],
        compiler_params=params(),
        cost_estimate=cost(2 * 128 * 256 * blocks * LO * feats_all // 4),
        name="gains",
    )(slab_rows, split_bin, x, bins, *pairs)


def make_pick(groups, tiles, feat_dev, feats):
    def kernel(split_ref, x_ref, g_ref, h_ref, o_ref, g_out, h_out, split_feature, rows_ref, gh_ref, sems):
        me = lax.axis_index("feat")
        split_copy = pltpu.make_async_copy(split_ref, split_feature, sems.at[3])
        g_copy = pltpu.make_async_copy(g_ref, gh_ref.at[0], sems.at[4])
        h_copy = pltpu.make_async_copy(h_ref, gh_ref.at[1], sems.at[5])
        split_copy.start()
        g_copy.start()
        h_copy.start()
        split_copy.wait()
        at8 = iota((8, LO), 0)
        work = []
        for n in range(3):
            local = split_feature[n] - me * feat_dev
            owned = (local >= 0) & (local < feat_dev)
            at = jnp.clip(local, 0, feat_dev - 1)
            s, f = at // feats, at % feats
            copy = pltpu.make_async_copy(x_ref.at[s, pl.ds(f // 8 * tiles, tiles)], rows_ref.at[n], sems.at[n])
            copy.start()
            work.append((copy, (at8 == f % 8) & owned))
        g_copy.wait()
        h_copy.wait()
        g_out[...] = gh_ref[0].astype(f32)
        h_out[...] = gh_ref[1].astype(f32)
        for n, (copy, mine) in enumerate(work):
            copy.wait()
            for i in range(tiles):
                row = jnp.sum(jnp.where(mine, rows_ref[n, i], 0.0), axis=0, keepdims=True)
                o_ref[n * tiles + i : n * tiles + i + 1, :] = row

    return kernel


def pick_rows(x, grad, hess, split_feature, groups, tiles, feat_dev):
    n_dp = x.shape[0]
    anywhere = pl.BlockSpec(memory_space=pl.ANY)
    vmem = pl.BlockSpec(memory_space=pltpu.VMEM)
    return pl.pallas_call(
        make_pick(groups, tiles, feat_dev, feat_dev // n_dp),
        out_shape=[pltpu.VMEM((rows * tiles, LO), f32) for rows in (3, 1, 1)],
        in_specs=[anywhere] * 4,
        out_specs=[vmem] * 3,
        scratch_shapes=[
            pltpu.SMEM((3,), i32),
            pltpu.VMEM((3, tiles, 8, LO), f32),
            pltpu.VMEM((2, tiles, LO), bf16),
            pltpu.SemaphoreType.DMA((6,)),
        ],
        name="pick",
    )(split_feature, x, grad.reshape(tiles, LO), hess.reshape(tiles, LO))


def swap(value, axis, size, step):
    return lax.ppermute(value, axis, [(s, s ^ step) for s in range(size)])


def make_shards(n_dp, n_feat):
    def shards(fine_values, grad, hess, slab_rows, split_feature, split_bin):
        feat_dev, row_dev = fine_values.shape
        feats, tiles = feat_dev // n_dp, row_dev // LO
        groups = (feats + 7) // 8
        me = lax.axis_index("dp")
        both = ("dp", "feat")
        x = fine_values.reshape(n_dp, feats, tiles, LO)
        x = jnp.pad(x, ((0, 0), (0, groups * 8 - feats), (0, 0), (0, 0)))
        x = x.reshape(n_dp, groups, 8, tiles, LO).swapaxes(2, 3).reshape(n_dp, groups * tiles, 8, LO)
        share, g, h = pick_rows(x, grad, hess, split_feature, groups, tiles, feat_dev)
        share = share + swap(share, "feat", n_feat, 1)
        share, g, block = lax.optimization_barrier((share, g, jnp.concatenate([share, g])))
        got = [swap(block, "dp", n_dp, 1)]
        for i in range(2, n_feat, 2):
            got.append(swap(share, "feat", n_feat, i))
            got.append(swap(share, both, n_dp * n_feat, n_feat + i))
        got = lax.optimization_barrier(got)
        mine, other, other_g = share, got[0][: 3 * tiles], got[0][3 * tiles :]
        for i in range(1, len(got), 2):
            mine, other = mine + got[i], other + got[i + 1]
        pair = jnp.stack([jnp.concatenate([mine, g]), jnp.concatenate([other, other_g])])
        pairs = [pair] + [swap(pair, "dp", n_dp, d) for d in range(2, n_dp, 2)]
        x = lax.all_to_all(x, "dp", 0, 0)
        h = jnp.stack([h, swap(h, "dp", n_dp, 1)])
        hs = [h] + [swap(h, "dp", n_dp, d) for d in range(2, n_dp, 2)]
        bins, h = find_bins(x, hs, slab_rows, split_bin, groups, tiles)
        gains = route_and_sum(h, pairs, bins, slab_rows, split_bin, feats, groups, tiles)
        pieces = [gains] + [None] * (n_dp - 1)
        for d in [*range(n_dp - 2, 0, -2), 1]:
            pieces[d] = swap(gains, "dp", n_dp, d)
        for d in range(3, n_dp, 2):
            pieces[d] = swap(pieces[d - 1], "dp", n_dp, 1)
        whole = jnp.zeros((7, feat_dev, BINS), f32)
        order = [4, 2] + [*range(6, n_dp, 2)] + [1] + [*range(3, n_dp, 2)]
        for d in [0] + [d for d in order if d < n_dp]:
            whole = lax.dynamic_update_slice_in_dim(whole, pieces[d], (me ^ d) * feats, 1)
        return whole

    return shards


def solution(mesh):
    return jax.shard_map(
        make_shards(mesh.shape["dp"], mesh.shape["feat"]),
        mesh=mesh,
        in_specs=(P("feat", "dp"), P("dp"), P("dp"), P(), P(), P()),
        out_specs=P(None, "feat", None),
        check_vma=False,
    )
```
